32 devices in a mesh: stream: 8 (over z, x), span: 4 (over y, core).
Axes of the slice: x: 2, y: 2, z: 4, core: 2. Of those that a mesh axis runs over, the one named last changes fastest.
Arguments:
- q_now: float32 [5, 128, 128, 128], P(None, 'stream', 'span'), may hold values from -4 to 4
- q_prev: float32 [5, 128, 128, 128], P(None, 'stream', 'span'), may hold values from -4 to 4
- jacobians: float32 [3, 5, 5], replicated, may hold values from -2.5 to 2.5
- fractions: float32 [3, 32, 1024], P(None, ('stream', 'span')), may hold values from 0 to 0.9
- send_blocks: int32 [32, 1024], P(('stream', 'span')), may hold values from -1 to 8191, as said below
- recv_blocks: int32 [32, 1024], P(('stream', 'span')), may hold values from -1 to 8191, as said below
Outputs:
- q_next: float32 [5, 128, 128, 128], P(None, 'stream', 'span')
The draws below stay inside these ranges and needn't reach their ends.
Inputs may be any that keep to these rules, and one draw needn't show every extreme that they name: In each row of send_blocks, the 32 slots to one destination hold valid brick indices first and -1 after them; a device sends only to devices whose streamwise rank differs from its own by at most 2, and to the device whose rank differs from its own by 16, which always receives exactly 32 valid slots from it; the busiest receivers get several times the mean. recv_blocks[r, s * 32 + k] is -1 exactly where send_blocks[s, r * 32 + k] is; the valid entries of one row are distinct.
All inputs are finite; a program needn't handle non-finite values.
Results may differ from the reference program's by a relative error of at most 0.0003.
Values sent between devices are 32-bit elements; how exact they have to be, the bound alone decides.
No kernel may reach another device: no remote copies, remote signals or barrier semaphores. Data moves between devices by JAX's collectives and lax.ppermute only.
A program may use at most 192 MiB of HBM per device.

```python
import jax
import jax.numpy as jnp
from jax import lax

CX = 16
CY = 32
CZ = 128
SLOT = 32
RANKS = 32
BLOCKS_DEV = 8192
NX = 128
NY = 128
NZ = 128
N_STREAM = 8
N_SPAN = 4


def field_values(key):
    shape = (5, NX, NY, NZ)
    values = jnp.clip(jax.random.normal(key, shape, jnp.float32), -4.0, 4.0)
    return values


def draw_q_now(key, part):
    return field_values(jax.random.fold_in(key, 21))


def draw_q_prev(key, part):
    return field_values(jax.random.fold_in(key, 22))


def donor_tables(key):
    ranks = jnp.arange(RANKS, dtype=jnp.int32)
    stream_rank = ranks // N_SPAN
    source_row = stream_rank[:, None]
    target_row = stream_rank[None, :]
    near = jnp.abs(source_row - target_row) <= 2
    opposite = (ranks[:, None] - ranks[None, :]) % RANKS == RANKS // 2
    base = jax.random.randint(jax.random.fold_in(key, 11), (RANKS, RANKS), 0, SLOT + 1)
    level = jnp.left_shift(jnp.int32(1), jax.random.randint(jax.random.fold_in(key, 12), (1, RANKS), 0, 4))
    counts = jnp.minimum(SLOT, base * level // 4)
    busiest = jax.random.randint(jax.random.fold_in(key, 13), (), 0, RANKS)
    counts = jnp.where(ranks[None, :] == busiest, SLOT, counts)
    counts = jnp.where(near, counts, 0)
    counts = jnp.where(opposite, SLOT, counts)
    live = jnp.arange(SLOT)[None, None, :] < counts[:, :, None]
    half_x = CX // 2
    face_depth = jax.random.randint(jax.random.fold_in(key, 16), (RANKS, RANKS, SLOT), 0, 2)
    anywhere_x = jax.random.randint(jax.random.fold_in(key, 17), (RANKS, RANKS, SLOT), 0, half_x)
    upstream = (source_row < target_row)[:, :, None]
    downstream = (source_row > target_row)[:, :, None]
    brick_x = jnp.where(upstream, half_x - 1 - face_depth, jnp.where(downstream, face_depth, anywhere_x))
    brick_y = jax.random.randint(jax.random.fold_in(key, 18), (RANKS, RANKS, SLOT), 0, CY // 2)
    brick_z = jax.random.randint(jax.random.fold_in(key, 19), (RANKS, RANKS, SLOT), 0, CZ // 2)
    picks = (brick_x * (CY // 2) + brick_y) * (CZ // 2) + brick_z
    sending = jnp.where(live, picks, -1).reshape(RANKS, RANKS * SLOT)
    row_keys = jax.random.split(jax.random.fold_in(key, 15), RANKS)
    orders = jax.vmap(lambda row_key: jax.random.permutation(row_key, BLOCKS_DEV)[:RANKS * SLOT])(row_keys)
    live_back = live.transpose(1, 0, 2).reshape(RANKS, RANKS * SLOT)
    receiving = jnp.where(live_back, orders, -1)
    return (sending.astype(jnp.int32), receiving.astype(jnp.int32))


def draw_send_blocks(key, part):
    return donor_tables(jax.random.fold_in(key, 7))[0]


def draw_recv_blocks(key, part):
    return donor_tables(jax.random.fold_in(key, 7))[1]


def levels(own_key, dims, pieces, least, high):
    gain, own = 1.0, jax.random.fold_in(own_key, 6)
    for dim, parts in pieces:
        steps = jnp.exp(jax.random.uniform(jax.random.fold_in(own, dim), (parts,), jnp.float32, least / len(pieces), high / len(pieces)))
        gain = gain * jnp.repeat(steps, dims[dim] // parts).reshape([-1 if axis == dim else 1 for axis in range(len(dims))])
    return gain


def gaussian(key, shape, spread, limit, held_as=jnp.bfloat16):
    result = spread * jax.random.normal(key, shape, jnp.float32)
    return jnp.clip(result, min=-limit, max=limit).astype(held_as)


def setup_inputs(seed: int = 0) -> dict:
    key_of = jax.random.split(jax.random.key(seed), 7)
    q_now = draw_q_now(jax.random.fold_in(key_of[6], 71), 0)
    q_prev = draw_q_prev(jax.random.fold_in(key_of[6], 71), 0)
    jacobians = gaussian(key_of[2], (3, 5, 5), 5 ** -0.5, 2.5, jnp.float32)
    fractions = jnp.clip(0.9 * jax.random.uniform(key_of[3], (3, RANKS, RANKS * SLOT), jnp.float32) ** levels(key_of[3], (3, RANKS, RANKS * SLOT), ((1, 32),), -0.2, 0.2), 0.0, 0.9)
    send_blocks = draw_send_blocks(jax.random.fold_in(key_of[6], 71), 0)
    recv_blocks = draw_recv_blocks(jax.random.fold_in(key_of[6], 71), 0)
    return dict(q_now=q_now, q_prev=q_prev, jacobians=jacobians, fractions=fractions, send_blocks=send_blocks, recv_blocks=recv_blocks)


FILTER_WEIGHTS = [1.0, -10.0, 45.0, -120.0, 210.0, -252.0, 210.0, -120.0, 45.0, -10.0, 1.0]
SIGMA = 0.6


def interpolate(values, fractions):
    slots = values.shape[1]
    cube = values.reshape(2, 2, 2, 10, slots)
    shift_x = fractions[0]
    shift_y = fractions[1]
    shift_z = fractions[2]
    lower = (1.0 - shift_x) * cube[0] + shift_x * cube[1]
    cube = jnp.stack([lower, cube[1]], 0)
    lower = (1.0 - shift_y) * cube[:, 0] + shift_y * cube[:, 1]
    cube = jnp.stack([lower, cube[:, 1]], 1)
    lower = (1.0 - shift_z) * cube[:, :, 0] + shift_z * cube[:, :, 1]
    cube = jnp.stack([lower, cube[:, :, 1]], 2)
    return cube.reshape(80, slots)


def place(bricks, values, targets):
    total = bricks.shape[1]
    where = jnp.where(targets >= 0, targets, total).astype(jnp.int32)
    return bricks.at[:, where].set(values, mode="drop")


def fourth(ext, axis):
    size = ext.shape[axis]

    def part(shift):
        return lax.slice_in_dim(ext, 2 + shift, size - 2 + shift, axis=axis)

    return (8.0 * (part(1) - part(-1)) - (part(2) - part(-2))) / 12.0


def rates(ext, jacobians):
    slope_x = fourth(ext[:, :, 2:-2, 2:-2], 1)
    slope_y = fourth(ext[:, 2:-2, :, 2:-2], 2)
    slope_z = fourth(ext[:, 2:-2, 2:-2, :], 3)
    high = lax.Precision.HIGHEST
    total = jnp.einsum("vw,wxyz->vxyz", jacobians[0], slope_x, precision=high)
    total = total + jnp.einsum("vw,wxyz->vxyz", jacobians[1], slope_y, precision=high)
    total = total + jnp.einsum("vw,wxyz->vxyz", jacobians[2], slope_z, precision=high)
    return -total


def tenth(ext, axis):
    size = ext.shape[axis]
    total = FILTER_WEIGHTS[0] * lax.slice_in_dim(ext, 0, size - 10, axis=axis)
    for offset in range(1, 11):
        total = total + FILTER_WEIGHTS[offset] * lax.slice_in_dim(ext, offset, size - 10 + offset, axis=axis)
    return total


def smooth(ext):
    along_x = tenth(ext[:, :, 5:-5, 5:-5], 1)
    along_y = tenth(ext[:, 5:-5, :, 5:-5], 2)
    along_z = tenth(ext[:, 5:-5, 5:-5, :], 3)
    centre = ext[:, 5:-5, 5:-5, 5:-5]
    return centre + (SIGMA / 1024.0) * (along_x + along_y + along_z)


def reference(q_now, q_prev, jacobians, fractions, send_blocks, recv_blocks):
    fields = jnp.concatenate([q_now, q_prev], 0)
    split = fields.reshape(10, N_STREAM, CX // 2, 2, N_SPAN, CY // 2, 2, CZ // 2, 2)
    bricks = split.transpose(1, 4, 3, 6, 8, 0, 2, 5, 7).reshape(RANKS, 80, BLOCKS_DEV)
    donors = jax.vmap(lambda brick, picks: brick[:, jnp.maximum(picks, 0).astype(jnp.int32)])(bricks, send_blocks)
    donors = donors.reshape(RANKS, 80, RANKS, SLOT).transpose(2, 1, 0, 3).reshape(RANKS, 80, RANKS * SLOT)
    fresh = jax.vmap(interpolate)(donors, fractions.transpose(1, 0, 2))
    bricks = jax.vmap(place)(bricks, fresh, recv_blocks)
    split = bricks.reshape(N_STREAM, N_SPAN, 2, 2, 2, 10, CX // 2, CY // 2, CZ // 2)
    fields = split.transpose(5, 0, 6, 2, 1, 7, 3, 8, 4).reshape(10, NX, NY, NZ)
    current = fields[:5]
    older = fields[5:]
    ext = jnp.pad(current, ((0, 0), (2, 2), (2, 2), (2, 2)))
    rhs = rates(ext, jacobians)
    pre = (4.0 * current - older + rhs) / 3.0
    return smooth(jnp.pad(pre, ((0, 0), (5, 5), (5, 5), (5, 5))))
```

```python
import functools

import jax
import jax.numpy as jnp
from jax import lax
from jax.experimental import pallas as pl
from jax.experimental.pallas import tpu as pltpu
from jax.sharding import PartitionSpec as P

TAPS = [-252.0, 210.0, -120.0, 45.0, -10.0, 1.0]
SIGMA = 0.6
REACH = 2
OFFSETS = 2 * REACH + 1
LANES = 128
VMEM_BYTES = 32 * 1024 * 1024
BIG_VMEM_BYTES = 60 * 1024 * 1024
STORE_BYTES = 40 * 1024 * 1024
VMEM = pl.BlockSpec(memory_space=pltpu.VMEM)
SMEM = pl.BlockSpec(memory_space=pltpu.SMEM)
HBM = pl.BlockSpec(memory_space=pltpu.HBM)
ANY = pl.BlockSpec(memory_space=pl.ANY)


def lane_pairs(rows):
    return lax.broadcasted_iota(jnp.int32, (rows, LANES), 1) >> 1


def pack_records(parts):
    lane = lax.broadcasted_iota(jnp.int32, (8, LANES), 1)
    first = jnp.where(lane < 80, parts[0], pltpu.roll(parts[3], 80, 1))
    second = jnp.where(lane < 112, pltpu.roll(parts[3], 32, 1), pltpu.roll(parts[2], 112, 1))
    second = jnp.where(lane < 80, parts[1], second)
    rest = pltpu.roll(parts[2], 112, 1)
    rest = jnp.where(lane < 64, rest, pltpu.roll(pltpu.roll(rest, 4, 0), 64, 1))
    return first[0:4], first[4:8], second[0:4], second[4:8], rest[0:4]


def unpack_records(pieces):
    lane = lax.broadcasted_iota(jnp.int32, (8, LANES), 1)
    first = jnp.concatenate(pieces[0:2], 0)
    second = jnp.concatenate(pieces[2:4], 0)
    rest = jnp.concatenate([pieces[4], pltpu.roll(pieces[4], 64, 1)], 0)
    third = jnp.where(lane < 16, pltpu.roll(second, 16, 1), pltpu.roll(rest, 16, 1))
    fourth = jnp.where(lane < 48, pltpu.roll(first, 48, 1), pltpu.roll(second, 96, 1))
    return first, second, third, fourth


def gather_kernel(
    send_hbm, now_hbm, old_hbm, bricks_hbm, near_hbm,
    fields_ref, bricks_ref, near_ref, turned_ref, stage_ref, send_ref, spot_ref, spots_ref, shelves_ref,
    load_sems, brick_sem, near_sems, table_sems,
    *, streams, spans, slot
):
    chans, size_x, size_y, size_z = now_hbm.shape
    half_y = size_y // 2
    deep = (size_z // 2).bit_length() - 1
    rows = 8 * chans
    columns = size_x // 2 * half_y
    here, across = lax.axis_index("stream"), lax.axis_index("span")

    def chunk(n, bx):
        src = (now_hbm, old_hbm)[n].at[:, pl.ds(2 * bx, 2)]
        dst = fields_ref.at[pl.ds(n * chans, chans), pl.ds(2 * bx, 2), pl.ds(8, size_y)]
        return pltpu.make_async_copy(src, dst, load_sems.at[n, bx])

    table = pltpu.make_async_copy(send_hbm, send_ref, table_sems.at[0])
    table.start()
    for bx in range(size_x // 2):
        chunk(0, bx).start()
        chunk(1, bx).start()
    table.wait()
    pick = jnp.maximum(send_ref[...], 0)
    column = pick >> deep
    group = (column * 171) >> 9
    spot_ref[0:1, :] = group * LANES + 2 * (pick & (size_z // 2 - 1))
    spot_ref[8:9, :] = (column - 3 * group) * LANES
    tables = [
        pltpu.make_async_copy(spot_ref.at[pl.ds(8 * n, 1)], dst, table_sems.at[n + 1])
        for n, dst in enumerate((spots_ref, shelves_ref))
    ]
    for copy in tables:
        copy.start()

    quarter = lax.broadcasted_iota(jnp.int32, (8, LANES), 0) >> 1

    blank = jnp.zeros((LANES - 3 * rows, LANES), jnp.float32)
    turned = 0
    for bx in range(size_x // 2):
        chunk(0, bx).wait()
        chunk(1, bx).wait()
        for by in range(half_y):
            for v in range(rows // 8):
                total = None
                for t in range(4):
                    c, dx = (4 * v + t) // 2, t % 2
                    start = 8 + 2 * by - 2 * t
                    part = fields_ref[c, 2 * bx + dx, start : start + 8, :]
                    total = part if total is None else jnp.where(quarter == t, part, total)
                bricks_ref[bx * half_y + by + 1, 8 * v + 8 : 8 * v + 16, :] = total
        ready = (bx + 1) * half_y
        while 3 * turned < columns and min(3 * turned + 3, columns) <= ready:
            parts = [bricks_ref[min(3 * turned + r + 1, columns), 8 : 8 + rows, :] for r in range(3)]
            turned_ref[turned * LANES : (turned + 1) * LANES, :] = jnp.concatenate([*parts, blank], 0).T
            turned += 1

    keep = pltpu.make_async_copy(bricks_ref, bricks_hbm.at[pl.ds(0, columns + 1)], brick_sem)
    keep.start()

    for copy in tables:
        copy.wait()
    lane = lax.broadcasted_iota(jnp.int32, (8, LANES), 1)

    def fetch(ranks, stage):
        stage[...] = jnp.zeros(stage.shape, jnp.float32)
        for h, rank in enumerate(ranks):
            for k in range(slot):
                spot = spots_ref[0, rank * slot + k]
                shelf = shelves_ref[0, rank * slot + k] + 2 * (slot * h + k)
                stage[pl.ds(shelf, 2), :] = turned_ref[pl.ds(spot, 2), :]
        for h, rank in enumerate(ranks):
            parts = []
            for q in range(4):
                start = 2 * slot * h + 16 * q
                even = [stage[pl.ds(r * LANES + start, 8, stride=2), :] for r in range(3)]
                odd = [stage[pl.ds(r * LANES + start + 1, 8, stride=2), :] for r in range(3)]
                even = even[0] + pltpu.roll(even[1], LANES - rows, 1) + pltpu.roll(even[2], LANES - 2 * rows, 1)
                odd = pltpu.roll(odd[0], rows, 1) + odd[1] + pltpu.roll(odd[2], LANES - rows, 1)
                parts.append(jnp.where(lane < rows, even, odd))
            for q, part in enumerate(pack_records(parts)):
                near_ref[rank, q] = part
            pltpu.make_async_copy(near_ref.at[rank], near_hbm.at[rank], near_sems.at[rank]).start()

    def finish(ranks):
        for rank in ranks:
            pltpu.make_async_copy(near_ref.at[rank], near_hbm.at[rank], near_sems.at[rank]).wait()

    opposite = lax.rem(here + streams // 2, streams) * spans + across
    per_offset = spans // 2

    def ranks_of(n):
        stream = here + (n // per_offset - REACH)
        first = stream * spans + 2 * lax.rem(n, per_offset)
        return jnp.logical_and(stream >= 0, stream < streams), (first, first + 1)

    @pl.loop(0, OFFSETS * per_offset)
    def _(n):
        inside, ranks = ranks_of(n)

        @pl.when(inside)
        def _():
            fetch(ranks, stage_ref.at[n])

    fetch((opposite,), stage_ref.at[OFFSETS * per_offset])

    @pl.loop(0, OFFSETS * per_offset)
    def _(n):
        inside, ranks = ranks_of(n)

        @pl.when(inside)
        def _():
            finish(ranks)

    finish((opposite,))
    keep.wait()


def band(weights, size):
    row = lax.broadcasted_iota(jnp.int32, (size, size), 0)
    col = lax.broadcasted_iota(jnp.int32, (size, size), 1)
    total = jnp.zeros((size, size), jnp.float32)
    for shift, weight in weights.items():
        total = jnp.where(row - col == shift, weight, total)
    return total.astype(jnp.bfloat16)


def along_z(values, matrix):
    high = values.astype(jnp.bfloat16)
    low = (values - high.astype(jnp.float32)).astype(jnp.bfloat16)
    total = jnp.dot(high, matrix, preferred_element_type=jnp.float32)
    return total + jnp.dot(low, matrix, preferred_element_type=jnp.float32)


def mix(jac_ref, d, vectors):
    result = []
    for v in range(len(vectors)):
        total = jac_ref[d, v, 0] * vectors[0]
        for w in range(1, len(vectors)):
            total = total + jac_ref[d, v, w] * vectors[w]
        result.append(total)
    return result


def edge_rows(now_ref, jac_ref, x, size_y):
    chans = now_ref.shape[0]
    tile = lax.broadcasted_iota(jnp.int32, (8, LANES), 0)
    vectors = []
    for c in range(chans):
        low = now_ref[c, x + 2, 8:16, :]
        top = now_ref[c, x + 2, size_y : size_y + 8, :]
        low_a, low_b = pltpu.roll(low, 7, 0), pltpu.roll(low, 6, 0)
        top_a, top_b = pltpu.roll(top, 1, 0), pltpu.roll(top, 2, 0)
        value = jnp.where(tile == 7, 8.0 * low_a - low_b, jnp.where(tile == 6, -low_b, 0.0))
        value = jnp.where(tile == 0, top_b - 8.0 * top_a, jnp.where(tile == 1, top_b, value))
        vectors.append(value)
    return mix(jac_ref, 1, vectors)


def mirrored(p, side, last):
    return p + side * (last - 2 * p)


def stream_sides():
    odd = lax.axis_index("stream") & 1
    return 1 - odd, odd


def span_pick(above, below):
    even = (lax.axis_index("span") & 1) == 0
    return jnp.where(even, above, below), jnp.where(even, below, above)


def edge_planes(now_ref, jac_ref, side, start, stop):
    chans = now_ref.shape[0]
    last = now_ref.shape[1] - 5

    def plane(p):
        return mix(jac_ref, 0, [now_ref[c, mirrored(p, side, last) + 2, 8 + start : 8 + stop, :] for c in range(chans)])

    first, second = plane(0), plane(1)
    sign = (1 - 2 * side).astype(jnp.float32)
    return [sign * (8.0 * first[c] - second[c]) for c in range(chans)], [-sign * first[c] for c in range(chans)]


def contribute(now_ref, jac_ref, side, out_ref):
    chans = now_ref.shape[0]
    size_y = now_ref.shape[2] - 16
    last = now_ref.shape[1] - 5
    planes = edge_planes(now_ref, jac_ref, side, 0, size_y)
    tile = lax.broadcasted_iota(jnp.int32, (8, LANES), 0)
    outer = jnp.logical_or(tile < 2, tile >= 6)
    mixed = [edge_rows(now_ref, jac_ref, mirrored(p, side, last), size_y) for p in range(5)]
    for c in range(chans):
        for p in range(2):
            out_ref[c, p * size_y : (p + 1) * size_y, :] = planes[p][c]
        for t in range(3):
            start = 2 * size_y + 8 * t
            if t < 2:
                second = mixed[2 * t + 1][c]
                second = jnp.where(tile < 4, pltpu.roll(second, 2, 0), pltpu.roll(second, 6, 0))
                out_ref[c, start : start + 8, :] = jnp.where(outer, mixed[2 * t][c], second)
            else:
                out_ref[c, start : start + 8, :] = jnp.where(outer, mixed[2 * t][c], 0.0)


def beyond(block, p, lower):
    if p % 2 == 0:
        return block
    return pltpu.roll(block, 6 if lower else 2, 0)


def cells(bricks_ref, c, dx, column):
    quarter = lax.broadcasted_iota(jnp.int32, (8, LANES), 0) >> 1
    total = None
    for s in range(4):
        start = 8 + 4 * c + 2 * dx - 2 * s
        part = bricks_ref[column + s + 1, pl.ds(start, 8), :]
        total = part if total is None else jnp.where(quarter == s, part, total)
    return total


def scatter_rows(recv_ref, fresh_ref, bricks_ref, first, last, *, streams, spans, slot):
    half_z = LANES // 2
    deep = half_z.bit_length() - 1
    here, across = lax.axis_index("stream"), lax.axis_index("span")
    per_offset = spans // 2
    pairs = lane_pairs(last - first)

    def scatter(unit, rank, count):
        values = fresh_ref[unit, first:last, :]
        for h in range(count):
            for k in range(slot):
                target = recv_ref[0, (rank + h) * slot + k]
                shift = (2 * target - 2 * (slot * h + k)) & (LANES - 1)
                moved = pltpu.roll(values, shift, 1)
                spot = bricks_ref.at[(target >> deep) + 1, pl.ds(8 + first, last - first), :]
                pltpu.store(spot, moved, mask=pairs == (target & (half_z - 1)))

    @pl.loop(0, OFFSETS * per_offset)
    def _(n):
        stream = here - (n // per_offset - REACH)
        rank = stream * spans + 2 * lax.rem(n, per_offset)

        @pl.when(jnp.logical_and(stream >= 0, stream < streams))
        def _():
            some = jnp.maximum(recv_ref[0, rank * slot], recv_ref[0, (rank + 1) * slot]) >= 0

            @pl.when(some)
            def _():
                scatter(n, rank, 2)

    scatter(OFFSETS * per_offset, lax.rem(here + streams // 2, streams) * spans + across, 1)


def fill_kernel(
    recv_hbm, frac_ref, jac_ref, base_hbm, near_ref,
    bricks_ref, fresh_ref, now_ref, first_add_ref, second_add_ref,
    spread_ref, flip_ref, recv_ref, sem, brick_sems,
    *, streams, spans, slot
):
    chans = now_ref.shape[0]
    size_x, size_y, size_z = now_ref.shape[1] - 4, now_ref.shape[2] - 16, now_ref.shape[3]
    half_y = size_y // 2
    rows = 8 * chans
    ranks = streams * spans // 2
    here, across = lax.axis_index("stream"), lax.axis_index("span")
    table = pltpu.make_async_copy(recv_hbm, recv_ref, sem)
    split = -(-rows // 16) * 8
    loads = []
    for n, (start, stop) in enumerate(((0, split), (split, rows))):
        inner = (pl.ds(1, size_x // 2 * half_y), pl.ds(8 + start, stop - start))
        loads.append(pltpu.make_async_copy(base_hbm.at[inner], bricks_ref.at[inner], brick_sems.at[n]))
        loads[n].start()
    table.start()

    source = lax.broadcasted_iota(jnp.int32, (LANES // 2, LANES), 0)
    copies = (source == lane_pairs(LANES // 2)).astype(jnp.float32)
    spread_ref[...] = jnp.dot(
        frac_ref[...], copies, preferred_element_type=jnp.float32, precision=lax.Precision.HIGHEST
    )
    cube = (rows // 8, 8, LANES)
    sub = lax.broadcasted_iota(jnp.int32, cube, 1)
    lane = lax.broadcasted_iota(jnp.int32, cube, 2)

    def interpolated(unit, rank, count, swap):
        flip = flip_ref.at[unit]
        for h in range(count):
            packed = [near_ref[rank + h, q] for q in range(5)]
            for q, part in enumerate(unpack_records(packed)):
                start = 2 * slot * h + 16 * q
                flip[pl.ds(start, 8, stride=2), :] = part
                flip[pl.ds(start + 1, 8, stride=2), :] = pltpu.roll(part, LANES - rows, 1)
        values = flip[...].T[0:rows].reshape(cube)
        shifts = []
        for d in range(3):
            line = spread_ref[pl.ds(d * ranks + (rank >> 1), 1), :]
            if swap:
                line = jnp.where((rank & 1) == 1, pltpu.roll(line, LANES // 2, 1), line)
            shifts.append(line.reshape(1, 1, LANES))
        low = (1.0 - shifts[0]) * values + shifts[0] * pltpu.roll(values, 6, 1)
        values = jnp.where((sub & 2) == 0, low, values)
        low = (1.0 - shifts[1]) * values + shifts[1] * pltpu.roll(values, 7, 1)
        values = jnp.where((sub & 1) == 0, low, values)
        low = (1.0 - shifts[2]) * values + shifts[2] * pltpu.roll(values, LANES - 1, 2)
        values = jnp.where((lane & 1) == 0, low, values)
        fresh_ref[unit] = values.reshape(rows, LANES)

    per_offset = spans // 2
    opposite = lax.rem(here + streams // 2, streams) * spans + across
    for d in range(OFFSETS):
        rank = jnp.clip(here - (d - REACH), 0, streams - 1) * spans
        for m in range(per_offset):
            interpolated(d * per_offset + m, rank + 2 * m, 2, False)
    interpolated(OFFSETS * per_offset, opposite, 1, True)

    table.wait()
    loads[0].wait()
    scatter_rows(recv_ref, fresh_ref, bricks_ref, 0, split, streams=streams, spans=spans, slot=slot)
    loads[1].wait()

    zeros = jnp.zeros((chans, size_y + 16, LANES), jnp.float32)
    for x in (0, 1, size_x + 2, size_x + 3):
        now_ref[:, x] = zeros
    rim = jnp.zeros((8, LANES), jnp.float32)

    @pl.loop(0, size_x // 2)
    def _(bx):
        for c in range(chans):
            for dx in range(2):
                now_ref[c, 2 * bx + dx + 2, 0:8, :] = rim
                for y in range(0, size_y, 8):
                    now_ref[c, 2 * bx + dx + 2, 8 + y : 16 + y, :] = cells(bricks_ref, c, dx, bx * half_y + y // 2)
                now_ref[c, 2 * bx + dx + 2, size_y + 8 : size_y + 16, :] = rim

    for side, add_ref in zip(stream_sides(), (first_add_ref, second_add_ref)):
        contribute(now_ref, jac_ref, side, add_ref)


def plane_pre(jac_ref, now_ref, bricks_ref, slope_ref, x, put):
    chans, size_y = now_ref.shape[0], now_ref.shape[2] - 16

    def part(c, dx, dy):
        return now_ref[c, x + 2 + dx, 8 + dy : 8 + size_y + dy, :]

    totals = []
    for c in range(chans):
        first = (x >> 1) * (size_y // 2)
        old = [cells(bricks_ref, chans + c, x & 1, first + y // 2) for y in range(0, size_y, 8)]
        totals.append(part(c, 0, 0) * (4.0 / 3.0) - jnp.concatenate(old, 0) * (1.0 / 3.0))
    for d in range(3):
        if d == 0:
            vectors = [8.0 * (part(c, 1, 0) - part(c, -1, 0)) - (part(c, 2, 0) - part(c, -2, 0)) for c in range(chans)]
        elif d == 1:
            vectors = [8.0 * (part(c, 0, 1) - part(c, 0, -1)) - (part(c, 0, 2) - part(c, 0, -2)) for c in range(chans)]
        else:
            vectors = [slope_ref[c, x] for c in range(chans)]
        totals = [total + value for total, value in zip(totals, mix(jac_ref, d, vectors))]
    for v in range(chans):
        put(v, totals[v])


def slope_planes(now_ref, slope_ref, start, count):
    chans, size_y = now_ref.shape[0], now_ref.shape[2] - 16
    slopes = band({1: 8.0, -1: -8.0, 2: -1.0, -2: 1.0}, now_ref.shape[3])
    for x in range(start, start + count):
        plane = now_ref[:, x + 2, 8 : 8 + size_y, :].reshape(chans * size_y, LANES)
        slope_ref[:, x] = along_z(plane, slopes).reshape(chans, size_y, LANES)


def edge_kernel(
    recv_hbm, jac_ref, now_ref, bricks_in, fresh_ref, bricks_ref, first_ref, second_ref, slope_ref, recv_ref, sem,
    *, streams, spans, slot
):
    del bricks_in
    table = pltpu.make_async_copy(recv_hbm, recv_ref, sem)
    table.start()
    chans, last = now_ref.shape[0], now_ref.shape[1] - 5
    slope_planes(now_ref, slope_ref, 0, 5)
    slope_planes(now_ref, slope_ref, last - 4, 5)
    table.wait()
    rows = 8 * chans
    split = -(-rows // 16) * 8
    scatter_rows(recv_ref, fresh_ref, bricks_ref, split, rows, streams=streams, spans=spans, slot=slot)
    for side, out_ref in zip(stream_sides(), (first_ref, second_ref)):

        @pl.loop(0, 5)
        def _(p):
            def put(v, value):
                out_ref[p, v] = value

            plane_pre(jac_ref, now_ref, bricks_ref, slope_ref, mirrored(p, side, last), put)


def tie_kernel(first_ref, left_in, right_in, left_ref, right_ref):
    del first_ref, left_in, right_in, left_ref, right_ref


def inner_kernel(
    jac_ref, now_ref, bricks_ref, first_ref, second_ref, first_mine_ref, second_mine_ref, first_add_ref, second_add_ref,
    pre_ref, first_rim_ref, second_rim_ref, slope_ref
):
    chans, size_x, size_y = now_ref.shape[0], now_ref.shape[1] - 4, now_ref.shape[2] - 16
    last = size_x - 1
    tile = lax.broadcasted_iota(jnp.int32, (8, LANES), 0)
    slope_planes(now_ref, slope_ref, 5, size_x - 10)

    def put(x, c, lower, upper):
        first_rim_ref[x, c], second_rim_ref[x, c] = span_pick(upper, lower)

    def put_rows(x, c, low, top, rows_low, rows_top):
        lower = jnp.where(tile == 5, 0.0, jnp.where(tile < 5, low, rows_low))
        upper = jnp.where(tile == 2, 0.0, jnp.where(tile >= 3, top, rows_top))
        put(x, c, lower, upper)

    refs = ((first_ref, first_mine_ref, first_add_ref), (second_ref, second_mine_ref, second_add_ref))
    sides = [(side, *ref) for side, ref in zip(stream_sides(), refs)]
    for side, src_ref, mine_ref, add_ref in sides:
        for c in range(chans):
            for p in range(5):
                low, top = src_ref[p, c, 0:8, :], src_ref[p, c, size_y - 8 : size_y, :]
                if p < 2:
                    low = low + add_ref[c, p * size_y : p * size_y + 8, :]
                    top = top + add_ref[c, (p + 1) * size_y - 8 : (p + 1) * size_y, :]
                start = 2 * size_y + 8 * (p // 2)
                mine = mine_ref[c, start : start + 8, :]
                put_rows(mirrored(p, side, last), c, low, top, beyond(mine, p, False), beyond(mine, p, True))

    for c in range(chans):
        for t in range(3):
            start = 2 * size_y + 8 * t
            blocks = first_add_ref[c, start : start + 8, :], second_add_ref[c, start : start + 8, :]
            left = jnp.where(sides[0][0] == 0, blocks[0], blocks[1])
            right = pltpu.roll(jnp.where(sides[0][0] == 0, blocks[1], blocks[0]), 4, 0)
            put(size_x + t, c, jnp.where(tile >= 4, left, right), jnp.where(tile < 4, left, right))

    @pl.loop(0, size_x - 10)
    def _(n):
        def keep(v, value):
            pre_ref[v, n] = value

        plane_pre(jac_ref, now_ref, bricks_ref, slope_ref, n + 5, keep)
        mixed = edge_rows(now_ref, jac_ref, n + 5, size_y)
        for c in range(chans):
            put_rows(n + 5, c, pre_ref[c, n, 0:8, :], pre_ref[c, n, size_y - 8 : size_y, :], mixed[c], mixed[c])


def radial_band(size_z):
    weights = {0: TAPS[0]}
    for s in range(1, 6):
        weights[s] = weights[-s] = TAPS[s]
    return band(weights, size_z)


def near_filter_kernel(
    pre_ref, first_ref, second_ref, first_add_ref, second_add_ref,
    first_rim_ref, second_rim_ref, first_from_ref, second_from_ref,
    out_ref, low_rows_ref, top_rows_ref, ext_ref, smooth_ref, *, spans
):
    chans, size_x, size_y, size_z = out_ref.shape
    across = lax.axis_index("span")
    last = size_x - 1
    top = size_y + 8
    has_lower = (across > 0).astype(jnp.float32)
    has_upper = (across < spans - 1).astype(jnp.float32)
    tile = lax.broadcasted_iota(jnp.int32, (8, LANES), 0)
    for x in [*range(5), *range(size_x + 5, size_x + 10)]:
        ext_ref[:, x] = jnp.zeros((chans, size_y + 16, LANES), jnp.float32)

    def fold(x, c, plane):
        up, low = span_pick(first_from_ref[x, c], second_from_ref[x, c])
        my_upper, my_lower = span_pick(first_rim_ref[x, c], second_rim_ref[x, c])
        ext_ref[c, x + 5, 16 : top - 8, :] = plane[8 : size_y - 8]
        ext_ref[c, x + 5, 8:16, :] = plane[0:8] + jnp.where(tile < 2, low, 0.0)
        ext_ref[c, x + 5, top - 8 : top, :] = plane[size_y - 8 :] + jnp.where(tile >= 6, up, 0.0)
        mine = has_lower * jnp.where(tile >= 6, my_lower, 0.0)
        ext_ref[c, x + 5, 0:8, :] = jnp.where(tile >= 3, low, 0.0) + mine
        mine = has_upper * jnp.where(tile < 2, my_upper, 0.0)
        ext_ref[c, x + 5, top : top + 8, :] = jnp.where(tile < 5, up, 0.0) + mine

    @pl.loop(0, size_x - 10)
    def _(n):
        for c in range(chans):
            fold(n + 5, c, pre_ref[c, n])

    refs = ((first_ref, first_add_ref), (second_ref, second_add_ref))
    for side, (src_ref, add_ref) in zip(stream_sides(), refs):
        for p in range(5):
            for c in range(chans):
                plane = src_ref[p, c]
                if p < 2:
                    plane = plane + add_ref[c, p * size_y : (p + 1) * size_y, :]
                fold(mirrored(p, side, last), c, plane)

    top_rows_ref[...], low_rows_ref[...] = span_pick(
        first_from_ref[size_x : size_x + 3], second_from_ref[size_x : size_x + 3]
    )
    radial = radial_band(size_z)

    @pl.loop(0, size_x, unroll=4)
    def _(x):
        plane = ext_ref[:, x + 5, 8:top, :].reshape(chans * size_y, LANES)
        smooth_ref[:, x] = along_z(plane, radial).reshape(chans, size_y, LANES)

    @pl.loop(0, size_x)
    def _(x):
        for c in range(chans):
            centre = ext_ref[c, x + 5, 8:top, :]
            total = smooth_ref[c, x] + (2.0 * TAPS[0]) * centre
            for s in range(1, 6):
                ring = ext_ref[c, x + 5 + s, 8:top, :] + ext_ref[c, x + 5 - s, 8:top, :]
                ring = ring + (ext_ref[c, x + 5, 8 + s : top + s, :] + ext_ref[c, x + 5, 8 - s : top - s, :])
                total = total + TAPS[s] * ring
            out_ref[c, x] = centre + (SIGMA / 1024.0) * total


def far_filter_kernel(
    part_ref, first_mine_ref, second_mine_ref, first_from_ref, second_from_ref, low_rows_ref, top_rows_ref,
    out_hbm, out_ref, middle_sem, sems, *, streams
):
    chans, size_x, size_y, _ = part_ref.shape
    tile = lax.broadcasted_iota(jnp.int32, (8, LANES), 0)
    here = lax.axis_index("stream")
    last = size_x - 1
    scale = SIGMA / 1024.0
    middle = pl.ds(5, size_x - 10)
    still = pltpu.make_async_copy(part_ref.at[:, middle], out_hbm.at[:, middle], middle_sem)
    still.start()

    sides = stream_sides()

    def put(n, c):
        planes = pl.ds(sides[n] * (size_x - 5), 5)
        return pltpu.make_async_copy(out_ref.at[c, planes], out_hbm.at[c, planes], sems.at[n, c])

    refs = ((first_mine_ref, first_from_ref), (second_mine_ref, second_from_ref))
    for n, (own_ref, from_ref) in enumerate(refs):
        side = sides[n]
        has = jnp.where(side == 0, here > 0, here < streams - 1).astype(jnp.float32)
        for c in range(chans):
            planes = []
            for p in range(5):
                plane = from_ref[p, c]
                if p < 2:
                    plane = plane + has * own_ref[c, p * size_y : (p + 1) * size_y, :]
                low, top = low_rows_ref[p // 2, c], top_rows_ref[p // 2, c]
                low = jnp.where(side == 1, pltpu.roll(low, 4, 0), low)
                top = jnp.where(side == 1, pltpu.roll(top, 4, 0), top)
                low = jnp.where(tile < 2, beyond(low, p, True), 0.0)
                top = jnp.where(tile >= 6, beyond(top, p, False), 0.0)
                plane = [plane[0:8] + low, plane[8 : size_y - 8], plane[size_y - 8 :] + top]
                planes.append(jnp.concatenate(plane, 0))
            for x in range(5):
                total = TAPS[x + 1] * planes[0]
                for p in range(1, 5 - x):
                    total = total + TAPS[x + 1 + p] * planes[p]
                at = mirrored(x, side, last)
                out_ref[c, at] = part_ref[c, at] + scale * total
            put(n, c).start()
    still.wait()
    for n in range(2):
        for c in range(chans):
            put(n, c).wait()


def params(size=VMEM_BYTES):
    return pltpu.CompilerParams(vmem_limit_bytes=size)


def per_device(q_now, q_prev, jacobians, fractions, send_blocks, recv_blocks):
    streams, spans = lax.axis_size("stream"), lax.axis_size("span")
    chans, size_x, size_y, size_z = q_now.shape
    slots = send_blocks.shape[1]
    slot = slots // (streams * spans)
    rows = 8 * chans
    columns = size_x // 2 * (size_y // 2)
    units = (OFFSETS * spans + 2) // 2
    f32 = jnp.float32
    shape = jax.ShapeDtypeStruct
    bricks = shape((columns + 1, rows + 16, LANES), f32)
    store = shape((STORE_BYTES // (4 * LANES * (rows + 16)), rows + 16, LANES), f32)
    packed = shape((streams * spans, 5, 4, LANES), f32)
    base, near = pl.pallas_call(
        functools.partial(gather_kernel, streams=streams, spans=spans, slot=slot),
        out_shape=[store, packed],
        in_specs=[HBM] * 3,
        out_specs=[HBM] * 2,
        scratch_shapes=[
            pltpu.VMEM((2 * chans, size_x, size_y + 16, LANES), f32),
            pltpu.VMEM(bricks.shape, f32),
            pltpu.VMEM(packed.shape, f32),
            pltpu.VMEM((-(-columns // 3) * LANES, LANES), f32),
            pltpu.VMEM((units, 3 * LANES, LANES), f32),
            pltpu.VMEM((1, slots), jnp.int32),
            pltpu.VMEM((16, slots), jnp.int32),
            pltpu.SMEM((1, slots), jnp.int32),
            pltpu.SMEM((1, slots), jnp.int32),
            pltpu.SemaphoreType.DMA((2, size_x // 2)),
            pltpu.SemaphoreType.DMA,
            pltpu.SemaphoreType.DMA((streams * spans,)),
            pltpu.SemaphoreType.DMA((3,)),
        ],
        compiler_params=params(BIG_VMEM_BYTES),
    )(send_blocks, q_now, q_prev)

    near = lax.all_to_all(near, ("stream", "span"), split_axis=0, concat_axis=0, tiled=True)

    jac = jacobians * (-1.0 / 36.0)
    frac_rows = 3 * streams * spans // 2
    add = shape((chans, 2 * size_y + 24, LANES), f32)
    bricks, fresh, now, first_mine, second_mine = pl.pallas_call(
        functools.partial(fill_kernel, streams=streams, spans=spans, slot=slot),
        out_shape=[
            bricks, shape((units, rows, LANES), f32), shape((chans, size_x + 4, size_y + 16, LANES), f32), add, add
        ],
        in_specs=[HBM, VMEM, SMEM, HBM, VMEM],
        out_specs=[VMEM] * 5,
        scratch_shapes=[
            pltpu.VMEM((frac_rows, LANES), f32),
            pltpu.VMEM((units, LANES, LANES), f32),
            pltpu.SMEM((1, slots), jnp.int32),
            pltpu.SemaphoreType.DMA,
            pltpu.SemaphoreType.DMA((2,)),
        ],
        compiler_params=params(),
    )(recv_blocks, fractions.reshape(frac_rows, LANES // 2), jac, base, near)

    def swaps(count):
        pairs = [[(i, i + 1) for i in range(start, count - 1, 2)] for start in range(2)]
        return [pair + [(b, a) for a, b in pair] for pair in pairs]

    along_stream, along_span = swaps(streams), swaps(spans)
    first_add = lax.ppermute(first_mine, "stream", along_stream[0])
    second_add = lax.ppermute(second_mine, "stream", along_stream[1])
    side = shape((5, chans, size_y, LANES), f32)
    rim = shape((size_x + 3, chans, 8, LANES), f32)
    slope = pltpu.VMEM((chans, size_x, size_y, LANES), f32)
    bricks, first, second = pl.pallas_call(
        functools.partial(edge_kernel, streams=streams, spans=spans, slot=slot),
        out_shape=[shape(bricks.shape, f32), side, side],
        in_specs=[HBM, SMEM] + [VMEM] * 3,
        out_specs=[VMEM] * 3,
        scratch_shapes=[slope, pltpu.SMEM((1, slots), jnp.int32), pltpu.SemaphoreType.DMA],
        input_output_aliases={3: 0},
        compiler_params=params(),
    )(recv_blocks, jac, now, bricks, fresh)
    first, second = pl.pallas_call(
        tie_kernel,
        out_shape=[side, side],
        in_specs=[ANY, VMEM, VMEM],
        out_specs=[VMEM] * 2,
        input_output_aliases={1: 0, 2: 1},
        compiler_params=params(),
    )(first_add, first, second)
    first_from = lax.ppermute(first, "stream", along_stream[0])
    second_from = lax.ppermute(second, "stream", along_stream[1])
    pre, first_rim, second_rim = pl.pallas_call(
        inner_kernel,
        out_shape=[shape((chans, size_x - 10, size_y, LANES), f32), rim, rim],
        in_specs=[SMEM] + [VMEM] * 8,
        out_specs=[VMEM] * 3,
        scratch_shapes=[slope],
        compiler_params=params(),
    )(jac, now, bricks, first, second, first_mine, second_mine, first_add, second_add)
    first_rows = lax.ppermute(first_rim, "span", along_span[0])
    second_rows = lax.ppermute(second_rim, "span", along_span[1])
    rows_shape = shape((3, chans, 8, LANES), f32)
    part, low_rows, top_rows = pl.pallas_call(
        functools.partial(near_filter_kernel, spans=spans),
        out_shape=[shape(q_now.shape, f32), rows_shape, rows_shape],
        in_specs=[VMEM] * 9,
        out_specs=[VMEM] * 3,
        scratch_shapes=[
            pltpu.VMEM((chans, size_x + 10, size_y + 16, LANES), f32),
            pltpu.VMEM(q_now.shape, f32),
        ],
        compiler_params=params(),
    )(pre, first, second, first_add, second_add, first_rim, second_rim, first_rows, second_rows)
    return pl.pallas_call(
        functools.partial(far_filter_kernel, streams=streams),
        out_shape=shape(q_now.shape, f32),
        in_specs=[VMEM] * 7,
        out_specs=HBM,
        scratch_shapes=[
            pltpu.VMEM(q_now.shape, f32),
            pltpu.SemaphoreType.DMA,
            pltpu.SemaphoreType.DMA((2, chans)),
        ],
        compiler_params=params(),
    )(part, first_mine, second_mine, first_from, second_from, low_rows, top_rows)


def solution(mesh):
    in_specs = (
        P(None, "stream", "span", None),
        P(None, "stream", "span", None),
        P(),
        P(None, ("stream", "span"), None),
        P(("stream", "span"), None),
        P(("stream", "span"), None),
    )
    out_specs = P(None, "stream", "span", None)
    return jax.shard_map(
        per_device, mesh=mesh, in_specs=in_specs, out_specs=out_specs, check_vma=False
    )
```

```python
import functools

import jax
import jax.numpy as jnp
from jax import lax
from jax.experimental import pallas as pl
from jax.experimental.pallas import tpu as pltpu
from jax.sharding import PartitionSpec as P

TAPS = [-252.0, 210.0, -120.0, 45.0, -10.0, 1.0]
SIGMA = 0.6
REACH = 2
OFFSETS = 2 * REACH + 1
LANES = 128
VMEM_BYTES = 32 * 1024 * 1024
BIG_VMEM_BYTES = 60 * 1024 * 1024
STORE_BYTES = 40 * 1024 * 1024
VMEM = pl.BlockSpec(memory_space=pltpu.VMEM)
SMEM = pl.BlockSpec(memory_space=pltpu.SMEM)
HBM = pl.BlockSpec(memory_space=pltpu.HBM)
ANY = pl.BlockSpec(memory_space=pl.ANY)


def lane_pairs(rows):
    return lax.broadcasted_iota(jnp.int32, (rows, LANES), 1) >> 1


def pack_records(parts):
    lane = lax.broadcasted_iota(jnp.int32, (8, LANES), 1)
    first = jnp.where(lane < 80, parts[0], pltpu.roll(parts[3], 80, 1))
    second = jnp.where(lane < 112, pltpu.roll(parts[3], 32, 1), pltpu.roll(parts[2], 112, 1))
    second = jnp.where(lane < 80, parts[1], second)
    rest = pltpu.roll(parts[2], 112, 1)
    rest = jnp.where(lane < 64, rest, pltpu.roll(pltpu.roll(rest, 4, 0), 64, 1))
    return first[0:4], first[4:8], second[0:4], second[4:8], rest[0:4]


def unpack_records(pieces):
    lane = lax.broadcasted_iota(jnp.int32, (8, LANES), 1)
    first = jnp.concatenate(pieces[0:2], 0)
    second = jnp.concatenate(pieces[2:4], 0)
    rest = jnp.concatenate([pieces[4], pltpu.roll(pieces[4], 64, 1)], 0)
    third = jnp.where(lane < 16, pltpu.roll(second, 16, 1), pltpu.roll(rest, 16, 1))
    fourth = jnp.where(lane < 48, pltpu.roll(first, 48, 1), pltpu.roll(second, 96, 1))
    return first, second, third, fourth


def gather_kernel(
    send_hbm, recv_hbm, now_hbm, old_hbm, bricks_hbm, near_hbm, tables_hbm,
    fields_ref, bricks_ref, near_ref, turned_ref, stage_ref, send_ref, recv_ref, spot_ref, spots_ref, shelves_ref,
    load_sems, brick_sem, near_sems, table_sems,
    *, streams, spans, slot
):
    chans, size_x, size_y, size_z = now_hbm.shape
    half_y = size_y // 2
    deep = (size_z // 2).bit_length() - 1
    rows = 8 * chans
    columns = size_x // 2 * half_y
    here, across = lax.axis_index("stream"), lax.axis_index("span")

    def chunk(n, bx):
        src = (now_hbm, old_hbm)[n].at[:, pl.ds(2 * bx, 2)]
        dst = fields_ref.at[pl.ds(n * chans, chans), pl.ds(2 * bx, 2), pl.ds(8, size_y)]
        return pltpu.make_async_copy(src, dst, load_sems.at[n, bx])

    table = pltpu.make_async_copy(send_hbm, send_ref, table_sems.at[0])
    table.start()
    received = pltpu.make_async_copy(recv_hbm, recv_ref, table_sems.at[3])
    received.start()
    for bx in range(size_x // 2):
        chunk(0, bx).start()
        chunk(1, bx).start()
    table.wait()
    pick = jnp.maximum(send_ref[...], 0)
    column = pick >> deep
    group = (column * 171) >> 9
    spot_ref[0:1, :] = group * LANES + 2 * (pick & (size_z // 2 - 1))
    spot_ref[8:9, :] = (column - 3 * group) * LANES
    tables = [
        pltpu.make_async_copy(spot_ref.at[pl.ds(8 * n, 1)], dst, table_sems.at[n + 1])
        for n, dst in enumerate((spots_ref, shelves_ref))
    ]
    for copy in tables:
        copy.start()
    received.wait()
    target = recv_ref[...]
    slots = lax.broadcasted_iota(jnp.int32, target.shape, 1)
    spot_ref[16:17, :] = (target >> deep) + 1
    spot_ref[24:25, :] = (2 * target - 2 * slots) & (LANES - 1)
    kept = [
        pltpu.make_async_copy(spot_ref.at[pl.ds(8 * n, 1)], dst, table_sems.at[n + 2])
        for n, dst in ((2, tables_hbm.at[0]), (3, tables_hbm.at[1]))
    ]
    for copy in kept:
        copy.start()

    quarter = lax.broadcasted_iota(jnp.int32, (8, LANES), 0) >> 1

    blank = jnp.zeros((LANES - 3 * rows, LANES), jnp.float32)
    turned = 0
    for bx in range(size_x // 2):
        chunk(0, bx).wait()
        chunk(1, bx).wait()
        for by in range(half_y):
            for v in range(rows // 8):
                total = None
                for t in range(4):
                    c, dx = (4 * v + t) // 2, t % 2
                    start = 8 + 2 * by - 2 * t
                    part = fields_ref[c, 2 * bx + dx, start : start + 8, :]
                    total = part if total is None else jnp.where(quarter == t, part, total)
                bricks_ref[bx * half_y + by + 1, 8 * v + 8 : 8 * v + 16, :] = total
        ready = (bx + 1) * half_y
        while 3 * turned < columns and min(3 * turned + 3, columns) <= ready:
            parts = [bricks_ref[min(3 * turned + r + 1, columns), 8 : 8 + rows, :] for r in range(3)]
            turned_ref[turned * LANES : (turned + 1) * LANES, :] = jnp.concatenate([*parts, blank], 0).T
            turned += 1

    keep = pltpu.make_async_copy(bricks_ref, bricks_hbm.at[pl.ds(0, columns + 1)], brick_sem)
    keep.start()

    for copy in tables:
        copy.wait()
    lane = lax.broadcasted_iota(jnp.int32, (8, LANES), 1)

    def fetch(ranks, stage):
        stage[...] = jnp.zeros(stage.shape, jnp.float32)
        for h, rank in enumerate(ranks):
            for k in range(slot):
                spot = spots_ref[0, rank * slot + k]
                shelf = shelves_ref[0, rank * slot + k] + 2 * (slot * h + k)
                stage[pl.ds(shelf, 2), :] = turned_ref[pl.ds(spot, 2), :]
        for h, rank in enumerate(ranks):
            parts = []
            for q in range(4):
                start = 2 * slot * h + 16 * q
                even = [stage[pl.ds(r * LANES + start, 8, stride=2), :] for r in range(3)]
                odd = [stage[pl.ds(r * LANES + start + 1, 8, stride=2), :] for r in range(3)]
                even = even[0] + pltpu.roll(even[1], LANES - rows, 1) + pltpu.roll(even[2], LANES - 2 * rows, 1)
                odd = pltpu.roll(odd[0], rows, 1) + odd[1] + pltpu.roll(odd[2], LANES - rows, 1)
                parts.append(jnp.where(lane < rows, even, odd))
            for q, part in enumerate(pack_records(parts)):
                near_ref[rank, q] = part
            pltpu.make_async_copy(near_ref.at[rank], near_hbm.at[rank], near_sems.at[rank]).start()

    def finish(ranks):
        for rank in ranks:
            pltpu.make_async_copy(near_ref.at[rank], near_hbm.at[rank], near_sems.at[rank]).wait()

    opposite = lax.rem(here + streams // 2, streams) * spans + across
    per_offset = spans // 2

    def ranks_of(n):
        stream = here + (n // per_offset - REACH)
        first = stream * spans + 2 * lax.rem(n, per_offset)
        return jnp.logical_and(stream >= 0, stream < streams), (first, first + 1)

    @pl.loop(0, OFFSETS * per_offset)
    def _(n):
        inside, ranks = ranks_of(n)

        @pl.when(inside)
        def _():
            fetch(ranks, stage_ref.at[n])

    fetch((opposite,), stage_ref.at[OFFSETS * per_offset])

    @pl.loop(0, OFFSETS * per_offset)
    def _(n):
        inside, ranks = ranks_of(n)

        @pl.when(inside)
        def _():
            finish(ranks)

    finish((opposite,))
    keep.wait()
    for copy in kept:
        copy.wait()


def band(weights, size):
    row = lax.broadcasted_iota(jnp.int32, (size, size), 0)
    col = lax.broadcasted_iota(jnp.int32, (size, size), 1)
    total = jnp.zeros((size, size), jnp.float32)
    for shift, weight in weights.items():
        total = jnp.where(row - col == shift, weight, total)
    return total.astype(jnp.bfloat16)


def along_z(values, matrix):
    high = values.astype(jnp.bfloat16)
    low = (values - high.astype(jnp.float32)).astype(jnp.bfloat16)
    total = jnp.dot(high, matrix, preferred_element_type=jnp.float32)
    return total + jnp.dot(low, matrix, preferred_element_type=jnp.float32)


def mix(jac_ref, d, vectors):
    result = []
    for v in range(len(vectors)):
        total = jac_ref[d, v, 0] * vectors[0]
        for w in range(1, len(vectors)):
            total = total + jac_ref[d, v, w] * vectors[w]
        result.append(total)
    return result


def edge_rows(now_ref, jac_ref, x, size_y):
    chans = now_ref.shape[0]
    tile = lax.broadcasted_iota(jnp.int32, (8, LANES), 0)
    vectors = []
    for c in range(chans):
        low = now_ref[c, x + 2, 8:16, :]
        top = now_ref[c, x + 2, size_y : size_y + 8, :]
        low_a, low_b = pltpu.roll(low, 7, 0), pltpu.roll(low, 6, 0)
        top_a, top_b = pltpu.roll(top, 1, 0), pltpu.roll(top, 2, 0)
        value = jnp.where(tile == 7, 8.0 * low_a - low_b, jnp.where(tile == 6, -low_b, 0.0))
        value = jnp.where(tile == 0, top_b - 8.0 * top_a, jnp.where(tile == 1, top_b, value))
        vectors.append(value)
    return mix(jac_ref, 1, vectors)


def mirrored(p, side, last):
    return p + side * (last - 2 * p)


def stream_sides():
    odd = lax.axis_index("stream") & 1
    return 1 - odd, odd


def span_pick(above, below):
    even = (lax.axis_index("span") & 1) == 0
    return jnp.where(even, above, below), jnp.where(even, below, above)


def edge_planes(now_ref, jac_ref, side, start, stop):
    chans = now_ref.shape[0]
    last = now_ref.shape[1] - 5

    def plane(p):
        return mix(jac_ref, 0, [now_ref[c, mirrored(p, side, last) + 2, 8 + start : 8 + stop, :] for c in range(chans)])

    first, second = plane(0), plane(1)
    sign = (1 - 2 * side).astype(jnp.float32)
    return [sign * (8.0 * first[c] - second[c]) for c in range(chans)], [-sign * first[c] for c in range(chans)]


def contribute(now_ref, jac_ref, side, out_ref):
    chans = now_ref.shape[0]
    size_y = now_ref.shape[2] - 16
    last = now_ref.shape[1] - 5
    planes = edge_planes(now_ref, jac_ref, side, 0, size_y)
    tile = lax.broadcasted_iota(jnp.int32, (8, LANES), 0)
    outer = jnp.logical_or(tile < 2, tile >= 6)
    mixed = [edge_rows(now_ref, jac_ref, mirrored(p, side, last), size_y) for p in range(5)]
    for c in range(chans):
        for p in range(2):
            out_ref[c, p * size_y : (p + 1) * size_y, :] = planes[p][c]
        for t in range(3):
            start = 2 * size_y + 8 * t
            if t < 2:
                second = mixed[2 * t + 1][c]
                second = jnp.where(tile < 4, pltpu.roll(second, 2, 0), pltpu.roll(second, 6, 0))
                out_ref[c, start : start + 8, :] = jnp.where(outer, mixed[2 * t][c], second)
            else:
                out_ref[c, start : start + 8, :] = jnp.where(outer, mixed[2 * t][c], 0.0)


def beyond(block, p, lower):
    if p % 2 == 0:
        return block
    return pltpu.roll(block, 6 if lower else 2, 0)


def cells(bricks_ref, c, dx, column):
    quarter = lax.broadcasted_iota(jnp.int32, (8, LANES), 0) >> 1
    total = None
    for s in range(4):
        start = 8 + 4 * c + 2 * dx - 2 * s
        part = bricks_ref[column + s + 1, pl.ds(start, 8), :]
        total = part if total is None else jnp.where(quarter == s, part, total)
    return total


def load_tables(tables_hbm, tables, sems):
    copies = [pltpu.make_async_copy(tables_hbm.at[n], dst, sems.at[n]) for n, dst in enumerate(tables)]
    for copy in copies:
        copy.start()
    return copies


def scatter_rows(tables, fresh_ref, bricks_ref, first, last, *, streams, spans, slot):
    columns_ref, shifts_ref = tables
    here, across = lax.axis_index("stream"), lax.axis_index("span")
    per_offset = spans // 2
    lane = lax.broadcasted_iota(jnp.int32, (last - first, LANES), 1)

    def scatter(unit, rank, count, turn):
        values = fresh_ref[unit, first:last, :]
        for h in range(count):
            for k in range(slot):
                shift = shifts_ref[0, (rank + h) * slot + k]
                if turn is not None:
                    shift = (shift + turn) & (LANES - 1)
                moved = pltpu.roll(values, shift, 1)
                spot = bricks_ref.at[columns_ref[0, (rank + h) * slot + k], pl.ds(8 + first, last - first), :]
                pltpu.store(spot, moved, mask=((lane - shift) & (LANES - 2)) == 2 * (slot * h + k))

    @pl.loop(0, OFFSETS * per_offset)
    def _(n):
        stream = here - (n // per_offset - REACH)
        rank = stream * spans + 2 * lax.rem(n, per_offset)

        @pl.when(jnp.logical_and(stream >= 0, stream < streams))
        def _():
            some = jnp.maximum(columns_ref[0, rank * slot], columns_ref[0, (rank + 1) * slot]) > 0

            @pl.when(some)
            def _():
                scatter(n, rank, 2, None)

    opposite = lax.rem(here + streams // 2, streams) * spans + across
    scatter(OFFSETS * per_offset, opposite, 1, 2 * slot * (opposite & 1))


def fill_kernel(
    tables_hbm, frac_ref, jac_ref, base_hbm, near_ref,
    bricks_ref, fresh_ref, now_ref, first_add_ref, second_add_ref,
    spread_ref, flip_ref, columns_ref, shifts_ref, table_sems, brick_sems,
    *, streams, spans, slot
):
    chans = now_ref.shape[0]
    size_x, size_y, size_z = now_ref.shape[1] - 4, now_ref.shape[2] - 16, now_ref.shape[3]
    half_y = size_y // 2
    rows = 8 * chans
    ranks = streams * spans // 2
    here, across = lax.axis_index("stream"), lax.axis_index("span")
    split = -(-rows // 16) * 8
    loads = []
    for n, (start, stop) in enumerate(((0, split), (split, rows))):
        inner = (pl.ds(1, size_x // 2 * half_y), pl.ds(8 + start, stop - start))
        loads.append(pltpu.make_async_copy(base_hbm.at[inner], bricks_ref.at[inner], brick_sems.at[n]))
        loads[n].start()
    tables = (columns_ref, shifts_ref)
    table_copies = load_tables(tables_hbm, tables, table_sems)

    source = lax.broadcasted_iota(jnp.int32, (LANES // 2, LANES), 0)
    copies = (source == lane_pairs(LANES // 2)).astype(jnp.float32)
    spread_ref[...] = jnp.dot(
        frac_ref[...], copies, preferred_element_type=jnp.float32, precision=lax.Precision.HIGHEST
    )
    cube = (rows // 8, 8, LANES)
    sub = lax.broadcasted_iota(jnp.int32, cube, 1)
    lane = lax.broadcasted_iota(jnp.int32, cube, 2)

    wide = lax.broadcasted_iota(jnp.int32, (8, LANES), 1)

    def turned(group, members):
        flip = flip_ref.at[group]
        for h in range(2):
            blocks = []
            for _, rank, count, _ in members:
                packed = [near_ref[rank + min(h, count - 1), q] for q in range(5)]
                blocks.append(unpack_records(packed))
            while len(blocks) < 3:
                blocks.append(blocks[-1])
            for q in range(4):
                a, b, c = (block[q] for block in blocks)
                start = 2 * slot * h + 16 * q
                even = jnp.where(wide < 2 * rows, pltpu.roll(b, rows, 1), pltpu.roll(c, 2 * rows, 1))
                flip[pl.ds(start, 8, stride=2), :] = jnp.where(wide < rows, a, even)
                odd = jnp.where(wide < 2 * rows, b, pltpu.roll(c, rows, 1))
                flip[pl.ds(start + 1, 8, stride=2), :] = jnp.where(wide < rows, pltpu.roll(a, LANES - rows, 1), odd)
        block = flip[...].T
        for n, (unit, rank, _, swap) in enumerate(members):
            interpolated(unit, rank, swap, block[n * rows : (n + 1) * rows].reshape(cube))

    def interpolated(unit, rank, swap, values):
        shifts = []
        for d in range(3):
            line = spread_ref[pl.ds(d * ranks + (rank >> 1), 1), :]
            if swap:
                line = jnp.where((rank & 1) == 1, pltpu.roll(line, LANES // 2, 1), line)
            shifts.append(line.reshape(1, 1, LANES))
        low = (1.0 - shifts[0]) * values + shifts[0] * pltpu.roll(values, 6, 1)
        values = jnp.where((sub & 2) == 0, low, values)
        low = (1.0 - shifts[1]) * values + shifts[1] * pltpu.roll(values, 7, 1)
        values = jnp.where((sub & 1) == 0, low, values)
        low = (1.0 - shifts[2]) * values + shifts[2] * pltpu.roll(values, LANES - 1, 2)
        values = jnp.where((lane & 1) == 0, low, values)
        fresh_ref[unit] = values.reshape(rows, LANES)

    per_offset = spans // 2
    opposite = lax.rem(here + streams // 2, streams) * spans + across
    members = []
    for d in range(OFFSETS):
        rank = jnp.clip(here - (d - REACH), 0, streams - 1) * spans
        for m in range(per_offset):
            members.append((d * per_offset + m, rank + 2 * m, 2, False))
    members.append((OFFSETS * per_offset, opposite, 1, True))
    for start in range(0, len(members), 3):
        turned(start // 3, members[start : start + 3])

    for copy in table_copies:
        copy.wait()
    loads[0].wait()
    scatter_rows(tables, fresh_ref, bricks_ref, 0, split, streams=streams, spans=spans, slot=slot)
    loads[1].wait()

    zeros = jnp.zeros((chans, size_y + 16, LANES), jnp.float32)
    for x in (0, 1, size_x + 2, size_x + 3):
        now_ref[:, x] = zeros
    rim = jnp.zeros((8, LANES), jnp.float32)

    @pl.loop(0, size_x // 2)
    def _(bx):
        for c in range(chans):
            for dx in range(2):
                now_ref[c, 2 * bx + dx + 2, 0:8, :] = rim
                for y in range(0, size_y, 8):
                    now_ref[c, 2 * bx + dx + 2, 8 + y : 16 + y, :] = cells(bricks_ref, c, dx, bx * half_y + y // 2)
                now_ref[c, 2 * bx + dx + 2, size_y + 8 : size_y + 16, :] = rim

    for side, add_ref in zip(stream_sides(), (first_add_ref, second_add_ref)):
        contribute(now_ref, jac_ref, side, add_ref)


def plane_pre(jac_ref, now_ref, bricks_ref, slope_ref, x, put):
    chans, size_y = now_ref.shape[0], now_ref.shape[2] - 16

    def part(c, dx, dy):
        return now_ref[c, x + 2 + dx, 8 + dy : 8 + size_y + dy, :]

    totals = []
    for c in range(chans):
        first = (x >> 1) * (size_y // 2)
        old = [cells(bricks_ref, chans + c, x & 1, first + y // 2) for y in range(0, size_y, 8)]
        totals.append(part(c, 0, 0) * (4.0 / 3.0) - jnp.concatenate(old, 0) * (1.0 / 3.0))
    for d in range(3):
        if d == 0:
            vectors = [8.0 * (part(c, 1, 0) - part(c, -1, 0)) - (part(c, 2, 0) - part(c, -2, 0)) for c in range(chans)]
        elif d == 1:
            vectors = [8.0 * (part(c, 0, 1) - part(c, 0, -1)) - (part(c, 0, 2) - part(c, 0, -2)) for c in range(chans)]
        else:
            vectors = [slope_ref[c, x] for c in range(chans)]
        totals = [total + value for total, value in zip(totals, mix(jac_ref, d, vectors))]
    for v in range(chans):
        put(v, totals[v])


def slope_planes(now_ref, slope_ref, start, count):
    chans, size_y = now_ref.shape[0], now_ref.shape[2] - 16
    slopes = band({1: 8.0, -1: -8.0, 2: -1.0, -2: 1.0}, now_ref.shape[3])
    for x in range(start, start + count):
        plane = now_ref[:, x + 2, 8 : 8 + size_y, :].reshape(chans * size_y, LANES)
        slope_ref[:, x] = along_z(plane, slopes).reshape(chans, size_y, LANES)


def edge_kernel(
    tables_hbm, jac_ref, now_ref, bricks_in, fresh_ref, first_mine_ref, second_mine_ref,
    bricks_ref, first_ref, second_ref, pre_ref, first_rim_ref, second_rim_ref,
    slope_ref, columns_ref, shifts_ref, table_sems,
    *, streams, spans, slot
):
    del bricks_in
    tables = (columns_ref, shifts_ref)
    copies = load_tables(tables_hbm, tables, table_sems)
    chans, size_x, size_y = now_ref.shape[0], now_ref.shape[1] - 4, now_ref.shape[2] - 16
    last = size_x - 1
    slope_planes(now_ref, slope_ref, 0, size_x)
    for copy in copies:
        copy.wait()
    rows = 8 * chans
    split = -(-rows // 16) * 8
    scatter_rows(tables, fresh_ref, bricks_ref, split, rows, streams=streams, spans=spans, slot=slot)
    for side, out_ref in zip(stream_sides(), (first_ref, second_ref)):

        @pl.loop(0, 5)
        def _(p):
            def put(v, value):
                out_ref[p, v] = value

            plane_pre(jac_ref, now_ref, bricks_ref, slope_ref, mirrored(p, side, last), put)


    tile = lax.broadcasted_iota(jnp.int32, (8, LANES), 0)

    def put_rows(x, c, low, top, rows_low, rows_top):
        lower = jnp.where(tile == 5, 0.0, jnp.where(tile < 5, low, rows_low))
        upper = jnp.where(tile == 2, 0.0, jnp.where(tile >= 3, top, rows_top))
        first_rim_ref[x, c], second_rim_ref[x, c] = span_pick(upper, lower)

    refs = ((first_ref, first_mine_ref), (second_ref, second_mine_ref))
    for side, (src_ref, mine_ref) in zip(stream_sides(), refs):
        for c in range(chans):
            for p in range(5):
                low, top = src_ref[p, c, 0:8, :], src_ref[p, c, size_y - 8 : size_y, :]
                start = 2 * size_y + 8 * (p // 2)
                mine = mine_ref[c, start : start + 8, :]
                put_rows(mirrored(p, side, last), c, low, top, beyond(mine, p, False), beyond(mine, p, True))

    @pl.loop(0, size_x - 10)
    def _(n):
        def keep(v, value):
            pre_ref[v, n] = value

        plane_pre(jac_ref, now_ref, bricks_ref, slope_ref, n + 5, keep)
        mixed = edge_rows(now_ref, jac_ref, n + 5, size_y)
        for c in range(chans):
            put_rows(n + 5, c, pre_ref[c, n, 0:8, :], pre_ref[c, n, size_y - 8 : size_y, :], mixed[c], mixed[c])


def tie_kernel(add_ref, plane_in, plane_ref):
    del add_ref, plane_in, plane_ref


def relay_kernel(first_add_ref, second_add_ref, first_in, second_in, first_rim_ref, second_rim_ref):
    del first_in, second_in
    chans = first_add_ref.shape[0]
    size_y = (first_add_ref.shape[1] - 24) // 2
    size_x = first_rim_ref.shape[0] - 3
    tile = lax.broadcasted_iota(jnp.int32, (8, LANES), 0)
    sides = stream_sides()
    for c in range(chans):
        for side, add_ref in zip(sides, (first_add_ref, second_add_ref)):
            for p in range(2):
                x = mirrored(p, side, size_x - 1)
                lower = jnp.where(tile < 5, add_ref[c, p * size_y : p * size_y + 8, :], 0.0)
                upper = jnp.where(tile >= 3, add_ref[c, (p + 1) * size_y - 8 : (p + 1) * size_y, :], 0.0)
                first, second = span_pick(upper, lower)
                first_rim_ref[x, c] += first
                second_rim_ref[x, c] += second
        for t in range(3):
            start = 2 * size_y + 8 * t
            blocks = first_add_ref[c, start : start + 8, :], second_add_ref[c, start : start + 8, :]
            left = jnp.where(sides[0] == 0, blocks[0], blocks[1])
            right = pltpu.roll(jnp.where(sides[0] == 0, blocks[1], blocks[0]), 4, 0)
            lower, upper = jnp.where(tile >= 4, left, right), jnp.where(tile < 4, left, right)
            first_rim_ref[size_x + t, c], second_rim_ref[size_x + t, c] = span_pick(upper, lower)


def radial_band(size_z):
    weights = {0: TAPS[0]}
    for s in range(1, 6):
        weights[s] = weights[-s] = TAPS[s]
    return band(weights, size_z)


def near_filter_kernel(
    pre_ref, first_ref, second_ref, first_add_ref, second_add_ref,
    first_rim_ref, second_rim_ref, first_from_ref, second_from_ref,
    out_ref, low_rows_ref, top_rows_ref, ext_ref, smooth_ref, *, spans
):
    chans, size_x, size_y, size_z = out_ref.shape
    across = lax.axis_index("span")
    last = size_x - 1
    top = size_y + 8
    has_lower = (across > 0).astype(jnp.float32)
    has_upper = (across < spans - 1).astype(jnp.float32)
    tile = lax.broadcasted_iota(jnp.int32, (8, LANES), 0)
    for x in [*range(5), *range(size_x + 5, size_x + 10)]:
        ext_ref[:, x] = jnp.zeros((chans, size_y + 16, LANES), jnp.float32)

    def fold(x, c, plane):
        up, low = span_pick(first_from_ref[x, c], second_from_ref[x, c])
        my_upper, my_lower = span_pick(first_rim_ref[x, c], second_rim_ref[x, c])
        ext_ref[c, x + 5, 16 : top - 8, :] = plane[8 : size_y - 8]
        ext_ref[c, x + 5, 8:16, :] = plane[0:8] + jnp.where(tile < 2, low, 0.0)
        ext_ref[c, x + 5, top - 8 : top, :] = plane[size_y - 8 :] + jnp.where(tile >= 6, up, 0.0)
        mine = has_lower * jnp.where(tile >= 6, my_lower, 0.0)
        ext_ref[c, x + 5, 0:8, :] = jnp.where(tile >= 3, low, 0.0) + mine
        mine = has_upper * jnp.where(tile < 2, my_upper, 0.0)
        ext_ref[c, x + 5, top : top + 8, :] = jnp.where(tile < 5, up, 0.0) + mine

    @pl.loop(0, size_x - 10)
    def _(n):
        for c in range(chans):
            fold(n + 5, c, pre_ref[c, n])

    refs = ((first_ref, first_add_ref), (second_ref, second_add_ref))
    for side, (src_ref, add_ref) in zip(stream_sides(), refs):
        for p in range(5):
            for c in range(chans):
                plane = src_ref[p, c]
                if p < 2:
                    plane = plane + add_ref[c, p * size_y : (p + 1) * size_y, :]
                fold(mirrored(p, side, last), c, plane)

    top_rows_ref[...], low_rows_ref[...] = span_pick(
        first_from_ref[size_x : size_x + 3], second_from_ref[size_x : size_x + 3]
    )
    radial = radial_band(size_z)

    @pl.loop(0, size_x, unroll=4)
    def _(x):
        plane = ext_ref[:, x + 5, 8:top, :].reshape(chans * size_y, LANES)
        smooth_ref[:, x] = along_z(plane, radial).reshape(chans, size_y, LANES)

    @pl.loop(0, size_x)
    def _(x):
        for c in range(chans):
            centre = ext_ref[c, x + 5, 8:top, :]
            total = smooth_ref[c, x] + (2.0 * TAPS[0]) * centre
            for s in range(1, 6):
                ring = ext_ref[c, x + 5 + s, 8:top, :] + ext_ref[c, x + 5 - s, 8:top, :]
                ring = ring + (ext_ref[c, x + 5, 8 + s : top + s, :] + ext_ref[c, x + 5, 8 - s : top - s, :])
                total = total + TAPS[s] * ring
            out_ref[c, x] = centre + (SIGMA / 1024.0) * total


def far_filter_kernel(
    part_ref, first_mine_ref, second_mine_ref, first_from_ref, second_from_ref, low_rows_ref, top_rows_ref,
    out_hbm, out_ref, middle_sem, sems, *, streams
):
    chans, size_x, size_y, _ = part_ref.shape
    tile = lax.broadcasted_iota(jnp.int32, (8, LANES), 0)
    here = lax.axis_index("stream")
    last = size_x - 1
    scale = SIGMA / 1024.0
    middle = pl.ds(5, size_x - 10)
    still = pltpu.make_async_copy(part_ref.at[:, middle], out_hbm.at[:, middle], middle_sem)
    still.start()

    sides = stream_sides()

    def put(n, c):
        planes = pl.ds(sides[n] * (size_x - 5), 5)
        return pltpu.make_async_copy(out_ref.at[c, planes], out_hbm.at[c, planes], sems.at[n, c])

    refs = ((first_mine_ref, first_from_ref), (second_mine_ref, second_from_ref))
    for n, (own_ref, from_ref) in enumerate(refs):
        side = sides[n]
        has = jnp.where(side == 0, here > 0, here < streams - 1).astype(jnp.float32)
        for c in range(chans):
            planes = []
            for p in range(5):
                plane = from_ref[p, c]
                if p < 2:
                    plane = plane + has * own_ref[c, p * size_y : (p + 1) * size_y, :]
                low, top = low_rows_ref[p // 2, c], top_rows_ref[p // 2, c]
                low = jnp.where(side == 1, pltpu.roll(low, 4, 0), low)
                top = jnp.where(side == 1, pltpu.roll(top, 4, 0), top)
                low = jnp.where(tile < 2, beyond(low, p, True), 0.0)
                top = jnp.where(tile >= 6, beyond(top, p, False), 0.0)
                plane = [plane[0:8] + low, plane[8 : size_y - 8], plane[size_y - 8 :] + top]
                planes.append(jnp.concatenate(plane, 0))
            for x in range(5):
                total = TAPS[x + 1] * planes[0]
                for p in range(1, 5 - x):
                    total = total + TAPS[x + 1 + p] * planes[p]
                at = mirrored(x, side, last)
                out_ref[c, at] = part_ref[c, at] + scale * total
            put(n, c).start()
    still.wait()
    for n in range(2):
        for c in range(chans):
            put(n, c).wait()


def params(size=VMEM_BYTES):
    return pltpu.CompilerParams(vmem_limit_bytes=size)


def per_device(q_now, q_prev, jacobians, fractions, send_blocks, recv_blocks):
    streams, spans = lax.axis_size("stream"), lax.axis_size("span")
    chans, size_x, size_y, size_z = q_now.shape
    slots = send_blocks.shape[1]
    slot = slots // (streams * spans)
    rows = 8 * chans
    columns = size_x // 2 * (size_y // 2)
    units = (OFFSETS * spans + 2) // 2
    f32 = jnp.float32
    shape = jax.ShapeDtypeStruct
    bricks = shape((columns + 1, rows + 16, LANES), f32)
    store = shape((STORE_BYTES // (4 * LANES * (rows + 16)), rows + 16, LANES), f32)
    packed = shape((streams * spans, 5, 4, LANES), f32)
    tables = shape((STORE_BYTES // (4 * slots), 1, slots), jnp.int32)
    base, near, tables = pl.pallas_call(
        functools.partial(gather_kernel, streams=streams, spans=spans, slot=slot),
        out_shape=[store, packed, tables],
        in_specs=[HBM] * 4,
        out_specs=[HBM] * 3,
        scratch_shapes=[
            pltpu.VMEM((2 * chans, size_x, size_y + 16, LANES), f32),
            pltpu.VMEM(bricks.shape, f32),
            pltpu.VMEM(packed.shape, f32),
            pltpu.VMEM((-(-columns // 3) * LANES, LANES), f32),
            pltpu.VMEM((units, 3 * LANES, LANES), f32),
            pltpu.VMEM((1, slots), jnp.int32),
            pltpu.VMEM((1, slots), jnp.int32),
            pltpu.VMEM((32, slots), jnp.int32),
            pltpu.SMEM((1, slots), jnp.int32),
            pltpu.SMEM((1, slots), jnp.int32),
            pltpu.SemaphoreType.DMA((2, size_x // 2)),
            pltpu.SemaphoreType.DMA,
            pltpu.SemaphoreType.DMA((streams * spans,)),
            pltpu.SemaphoreType.DMA((6,)),
        ],
        compiler_params=params(BIG_VMEM_BYTES),
    )(send_blocks, recv_blocks, q_now, q_prev)

    near = lax.all_to_all(near, ("stream", "span"), split_axis=0, concat_axis=0, tiled=True)

    jac = jacobians * (-1.0 / 36.0)
    frac_rows = 3 * streams * spans // 2
    add = shape((chans, 2 * size_y + 24, LANES), f32)
    bricks, fresh, now, first_mine, second_mine = pl.pallas_call(
        functools.partial(fill_kernel, streams=streams, spans=spans, slot=slot),
        out_shape=[
            bricks, shape((units, rows, LANES), f32), shape((chans, size_x + 4, size_y + 16, LANES), f32), add, add
        ],
        in_specs=[HBM, VMEM, SMEM, HBM, VMEM],
        out_specs=[VMEM] * 5,
        scratch_shapes=[
            pltpu.VMEM((frac_rows, LANES), f32),
            pltpu.VMEM((-(-units // 3), LANES, LANES), f32),
            pltpu.SMEM((1, slots), jnp.int32),
            pltpu.SMEM((1, slots), jnp.int32),
            pltpu.SemaphoreType.DMA((2,)),
            pltpu.SemaphoreType.DMA((2,)),
        ],
        compiler_params=params(),
    )(tables, fractions.reshape(frac_rows, LANES // 2), jac, base, near)

    def swaps(count):
        pairs = [[(i, i + 1) for i in range(start, count - 1, 2)] for start in range(2)]
        return [pair + [(b, a) for a, b in pair] for pair in pairs]

    along_stream, along_span = swaps(streams), swaps(spans)
    first_add = lax.ppermute(first_mine, "stream", along_stream[0])
    second_add = lax.ppermute(second_mine, "stream", along_stream[1])
    side = shape((5, chans, size_y, LANES), f32)
    rim = shape((size_x + 3, chans, 8, LANES), f32)
    _, first, second, pre, first_rim, second_rim = pl.pallas_call(
        functools.partial(edge_kernel, streams=streams, spans=spans, slot=slot),
        out_shape=[
            shape(bricks.shape, f32), side, side, shape((chans, size_x - 10, size_y, LANES), f32), rim, rim
        ],
        in_specs=[HBM, SMEM] + [VMEM] * 5,
        out_specs=[VMEM] * 6,
        scratch_shapes=[
            pltpu.VMEM((chans, size_x, size_y, LANES), f32),
            pltpu.SMEM((1, slots), jnp.int32),
            pltpu.SMEM((1, slots), jnp.int32),
            pltpu.SemaphoreType.DMA((2,)),
        ],
        input_output_aliases={3: 0},
        compiler_params=params(),
    )(tables, jac, now, bricks, fresh, first_mine, second_mine)
    second = pl.pallas_call(
        tie_kernel,
        out_shape=side,
        in_specs=[ANY, VMEM],
        out_specs=VMEM,
        input_output_aliases={1: 0},
        compiler_params=params(),
    )(first_add, second)
    first_from = lax.ppermute(first, "stream", along_stream[0])
    second_from = lax.ppermute(second, "stream", along_stream[1])
    first_rim, second_rim = pl.pallas_call(
        relay_kernel,
        out_shape=[rim, rim],
        in_specs=[VMEM] * 4,
        out_specs=[VMEM] * 2,
        input_output_aliases={2: 0, 3: 1},
        compiler_params=params(),
    )(first_add, second_add, first_rim, second_rim)
    first_rows = lax.ppermute(first_rim, "span", along_span[0])
    second_rows = lax.ppermute(second_rim, "span", along_span[1])
    rows_shape = shape((3, chans, 8, LANES), f32)
    part, low_rows, top_rows = pl.pallas_call(
        functools.partial(near_filter_kernel, spans=spans),
        out_shape=[shape(q_now.shape, f32), rows_shape, rows_shape],
        in_specs=[VMEM] * 9,
        out_specs=[VMEM] * 3,
        scratch_shapes=[
            pltpu.VMEM((chans, size_x + 10, size_y + 16, LANES), f32),
            pltpu.VMEM(q_now.shape, f32),
        ],
        compiler_params=params(),
    )(pre, first, second, first_add, second_add, first_rim, second_rim, first_rows, second_rows)
    return pl.pallas_call(
        functools.partial(far_filter_kernel, streams=streams),
        out_shape=shape(q_now.shape, f32),
        in_specs=[VMEM] * 7,
        out_specs=HBM,
        scratch_shapes=[
            pltpu.VMEM(q_now.shape, f32),
            pltpu.SemaphoreType.DMA,
            pltpu.SemaphoreType.DMA((2, chans)),
        ],
        compiler_params=params(),
    )(part, first_mine, second_mine, first_from, second_from, low_rows, top_rows)


def solution(mesh):
    in_specs = (
        P(None, "stream", "span", None),
        P(None, "stream", "span", None),
        P(),
        P(None, ("stream", "span"), None),
        P(("stream", "span"), None),
        P(("stream", "span"), None),
    )
    out_specs = P(None, "stream", "span", None)
    return jax.shard_map(
        per_device, mesh=mesh, in_specs=in_specs, out_specs=out_specs, check_vma=False
    )
```

```python
import functools

import jax
import jax.numpy as jnp
from jax import lax
from jax.experimental import pallas as pl
from jax.experimental.pallas import tpu as pltpu
from jax.sharding import PartitionSpec as P

TAPS = [-252.0, 210.0, -120.0, 45.0, -10.0, 1.0]
SIGMA = 0.6
REACH = 2
OFFSETS = 2 * REACH + 1
LANES = 128
VMEM_BYTES = 32 * 1024 * 1024
BIG_VMEM_BYTES = 60 * 1024 * 1024
STORE_BYTES = 40 * 1024 * 1024
VMEM = pl.BlockSpec(memory_space=pltpu.VMEM)
SMEM = pl.BlockSpec(memory_space=pltpu.SMEM)
HBM = pl.BlockSpec(memory_space=pltpu.HBM)
ANY = pl.BlockSpec(memory_space=pl.ANY)


def lane_pairs(rows):
    return lax.broadcasted_iota(jnp.int32, (rows, LANES), 1) >> 1


def pack_records(parts):
    lane = lax.broadcasted_iota(jnp.int32, (8, LANES), 1)
    first = jnp.where(lane < 80, parts[0], pltpu.roll(parts[3], 80, 1))
    second = jnp.where(lane < 112, pltpu.roll(parts[3], 32, 1), pltpu.roll(parts[2], 112, 1))
    second = jnp.where(lane < 80, parts[1], second)
    rest = pltpu.roll(parts[2], 112, 1)
    rest = jnp.where(lane < 64, rest, pltpu.roll(pltpu.roll(rest, 4, 0), 64, 1))
    return first[0:4], first[4:8], second[0:4], second[4:8], rest[0:4]


def unpack_records(pieces):
    lane = lax.broadcasted_iota(jnp.int32, (8, LANES), 1)
    first = jnp.concatenate(pieces[0:2], 0)
    second = jnp.concatenate(pieces[2:4], 0)
    rest = jnp.concatenate([pieces[4], pltpu.roll(pieces[4], 64, 1)], 0)
    third = jnp.where(lane < 16, pltpu.roll(second, 16, 1), pltpu.roll(rest, 16, 1))
    fourth = jnp.where(lane < 48, pltpu.roll(first, 48, 1), pltpu.roll(second, 96, 1))
    return first, second, third, fourth


def gather_kernel(
    send_hbm, recv_hbm, now_hbm, old_hbm, bricks_hbm, near_hbm, tables_hbm,
    fields_ref, bricks_ref, near_ref, turned_ref, stage_ref, send_ref, recv_ref, spot_ref, spots_ref, shelves_ref,
    load_sems, brick_sem, near_sems, table_sems,
    *, streams, spans, slot
):
    chans, size_x, size_y, size_z = now_hbm.shape
    half_y = size_y // 2
    deep = (size_z // 2).bit_length() - 1
    rows = 8 * chans
    columns = size_x // 2 * half_y
    here, across = lax.axis_index("stream"), lax.axis_index("span")

    def chunk(n, bx):
        src = (now_hbm, old_hbm)[n].at[:, pl.ds(2 * bx, 2)]
        dst = fields_ref.at[pl.ds(n * chans, chans), pl.ds(2 * bx, 2), pl.ds(8, size_y)]
        return pltpu.make_async_copy(src, dst, load_sems.at[n, bx])

    table = pltpu.make_async_copy(send_hbm, send_ref, table_sems.at[0])
    table.start()
    received = pltpu.make_async_copy(recv_hbm, recv_ref, table_sems.at[3])
    received.start()
    for bx in range(size_x // 2):
        chunk(0, bx).start()
        chunk(1, bx).start()
    table.wait()
    pick = jnp.maximum(send_ref[...], 0)
    column = pick >> deep
    group = (column * 171) >> 9
    spot_ref[0:1, :] = group * LANES + 2 * (pick & (size_z // 2 - 1))
    spot_ref[8:9, :] = (column - 3 * group) * LANES
    tables = [
        pltpu.make_async_copy(spot_ref.at[pl.ds(8 * n, 1)], dst, table_sems.at[n + 1])
        for n, dst in enumerate((spots_ref, shelves_ref))
    ]
    for copy in tables:
        copy.start()
    received.wait()
    target = recv_ref[...]
    slots = lax.broadcasted_iota(jnp.int32, target.shape, 1)
    spot_ref[16:17, :] = (target >> deep) + 1
    spot_ref[24:25, :] = (2 * target - 2 * slots) & (LANES - 1)
    kept = [
        pltpu.make_async_copy(spot_ref.at[pl.ds(8 * n, 1)], dst, table_sems.at[n + 2])
        for n, dst in ((2, tables_hbm.at[0]), (3, tables_hbm.at[1]))
    ]
    for copy in kept:
        copy.start()

    quarter = lax.broadcasted_iota(jnp.int32, (8, LANES), 0) >> 1

    blank = jnp.zeros((LANES - 3 * rows, LANES), jnp.float32)
    turned = 0
    for bx in range(size_x // 2):
        chunk(0, bx).wait()
        chunk(1, bx).wait()
        for by in range(half_y):
            for v in range(rows // 8):
                total = None
                for t in range(4):
                    c, dx = (4 * v + t) // 2, t % 2
                    start = 8 + 2 * by - 2 * t
                    part = fields_ref[c, 2 * bx + dx, start : start + 8, :]
                    total = part if total is None else jnp.where(quarter == t, part, total)
                bricks_ref[bx * half_y + by + 1, 8 * v + 8 : 8 * v + 16, :] = total
        ready = (bx + 1) * half_y
        while 3 * turned < columns and min(3 * turned + 3, columns) <= ready:
            parts = [bricks_ref[min(3 * turned + r + 1, columns), 8 : 8 + rows, :] for r in range(3)]
            turned_ref[turned * LANES : (turned + 1) * LANES, :] = jnp.concatenate([*parts, blank], 0).T
            turned += 1

    keep = pltpu.make_async_copy(bricks_ref, bricks_hbm.at[pl.ds(0, columns + 1)], brick_sem)
    keep.start()

    for copy in tables:
        copy.wait()
    lane = lax.broadcasted_iota(jnp.int32, (8, LANES), 1)

    def fetch(ranks, stage):
        stage[...] = jnp.zeros(stage.shape, jnp.float32)
        for h, rank in enumerate(ranks):
            for k in range(slot):
                spot = spots_ref[0, rank * slot + k]
                shelf = shelves_ref[0, rank * slot + k] + 2 * (slot * h + k)
                stage[pl.ds(shelf, 2), :] = turned_ref[pl.ds(spot, 2), :]
        for h, rank in enumerate(ranks):
            parts = []
            for q in range(4):
                start = 2 * slot * h + 16 * q
                even = [stage[pl.ds(r * LANES + start, 8, stride=2), :] for r in range(3)]
                odd = [stage[pl.ds(r * LANES + start + 1, 8, stride=2), :] for r in range(3)]
                even = even[0] + pltpu.roll(even[1], LANES - rows, 1) + pltpu.roll(even[2], LANES - 2 * rows, 1)
                odd = pltpu.roll(odd[0], rows, 1) + odd[1] + pltpu.roll(odd[2], LANES - rows, 1)
                parts.append(jnp.where(lane < rows, even, odd))
            for q, part in enumerate(pack_records(parts)):
                near_ref[rank, q] = part
            pltpu.make_async_copy(near_ref.at[rank], near_hbm.at[rank], near_sems.at[rank]).start()

    def finish(ranks):
        for rank in ranks:
            pltpu.make_async_copy(near_ref.at[rank], near_hbm.at[rank], near_sems.at[rank]).wait()

    opposite = lax.rem(here + streams // 2, streams) * spans + across
    per_offset = spans // 2

    def ranks_of(n):
        stream = here + (n // per_offset - REACH)
        first = stream * spans + 2 * lax.rem(n, per_offset)
        return jnp.logical_and(stream >= 0, stream < streams), (first, first + 1)

    @pl.loop(0, OFFSETS * per_offset)
    def _(n):
        inside, ranks = ranks_of(n)

        @pl.when(inside)
        def _():
            fetch(ranks, stage_ref.at[n])

    fetch((opposite,), stage_ref.at[OFFSETS * per_offset])

    @pl.loop(0, OFFSETS * per_offset)
    def _(n):
        inside, ranks = ranks_of(n)

        @pl.when(inside)
        def _():
            finish(ranks)

    finish((opposite,))
    keep.wait()
    for copy in kept:
        copy.wait()


def band(weights, size):
    row = lax.broadcasted_iota(jnp.int32, (size, size), 0)
    col = lax.broadcasted_iota(jnp.int32, (size, size), 1)
    total = jnp.zeros((size, size), jnp.float32)
    for shift, weight in weights.items():
        total = jnp.where(row - col == shift, weight, total)
    return total.astype(jnp.bfloat16)


def along_z(values, matrix):
    high = values.astype(jnp.bfloat16)
    low = (values - high.astype(jnp.float32)).astype(jnp.bfloat16)
    total = jnp.dot(high, matrix, preferred_element_type=jnp.float32)
    return total + jnp.dot(low, matrix, preferred_element_type=jnp.float32)


def mix(jac_ref, d, vectors):
    result = []
    for v in range(len(vectors)):
        total = jac_ref[d, v, 0] * vectors[0]
        for w in range(1, len(vectors)):
            total = total + jac_ref[d, v, w] * vectors[w]
        result.append(total)
    return result


def edge_rows(now_ref, jac_ref, x, size_y):
    chans = now_ref.shape[0]
    tile = lax.broadcasted_iota(jnp.int32, (8, LANES), 0)
    vectors = []
    for c in range(chans):
        low = now_ref[c, x + 2, 8:16, :]
        top = now_ref[c, x + 2, size_y : size_y + 8, :]
        low_a, low_b = pltpu.roll(low, 7, 0), pltpu.roll(low, 6, 0)
        top_a, top_b = pltpu.roll(top, 1, 0), pltpu.roll(top, 2, 0)
        value = jnp.where(tile == 7, 8.0 * low_a - low_b, jnp.where(tile == 6, -low_b, 0.0))
        value = jnp.where(tile == 0, top_b - 8.0 * top_a, jnp.where(tile == 1, top_b, value))
        vectors.append(value)
    return mix(jac_ref, 1, vectors)


def mirrored(p, side, last):
    return p + side * (last - 2 * p)


def stream_sides():
    odd = lax.axis_index("stream") & 1
    return 1 - odd, odd


def span_pick(above, below):
    even = (lax.axis_index("span") & 1) == 0
    return jnp.where(even, above, below), jnp.where(even, below, above)


def edge_planes(now_ref, jac_ref, side, start, stop):
    chans = now_ref.shape[0]
    last = now_ref.shape[1] - 5

    def plane(p):
        return mix(jac_ref, 0, [now_ref[c, mirrored(p, side, last) + 2, 8 + start : 8 + stop, :] for c in range(chans)])

    first, second = plane(0), plane(1)
    sign = (1 - 2 * side).astype(jnp.float32)
    return [sign * (8.0 * first[c] - second[c]) for c in range(chans)], [-sign * first[c] for c in range(chans)]


def contribute(now_ref, jac_ref, side, out_ref):
    chans = now_ref.shape[0]
    size_y = now_ref.shape[2] - 16
    last = now_ref.shape[1] - 5
    planes = edge_planes(now_ref, jac_ref, side, 0, size_y)
    tile = lax.broadcasted_iota(jnp.int32, (8, LANES), 0)
    outer = jnp.logical_or(tile < 2, tile >= 6)
    mixed = [edge_rows(now_ref, jac_ref, mirrored(p, side, last), size_y) for p in range(5)]
    for c in range(chans):
        for p in range(2):
            out_ref[c, p * size_y : (p + 1) * size_y, :] = planes[p][c]
        for t in range(3):
            start = 2 * size_y + 8 * t
            if t < 2:
                second = mixed[2 * t + 1][c]
                second = jnp.where(tile < 4, pltpu.roll(second, 2, 0), pltpu.roll(second, 6, 0))
                out_ref[c, start : start + 8, :] = jnp.where(outer, mixed[2 * t][c], second)
            else:
                out_ref[c, start : start + 8, :] = jnp.where(outer, mixed[2 * t][c], 0.0)


def beyond(block, p, lower):
    if p % 2 == 0:
        return block
    return pltpu.roll(block, 6 if lower else 2, 0)


def cells(bricks_ref, c, dx, column):
    quarter = lax.broadcasted_iota(jnp.int32, (8, LANES), 0) >> 1
    total = None
    for s in range(4):
        start = 8 + 4 * c + 2 * dx - 2 * s
        part = bricks_ref[column + s + 1, pl.ds(start, 8), :]
        total = part if total is None else jnp.where(quarter == s, part, total)
    return total


def load_tables(tables_hbm, tables, sems):
    copies = [pltpu.make_async_copy(tables_hbm.at[n], dst, sems.at[n]) for n, dst in enumerate(tables)]
    for copy in copies:
        copy.start()
    return copies


def scatter_rows(tables, fresh_ref, bricks_ref, first, last, *, streams, spans, slot):
    columns_ref, shifts_ref = tables
    here, across = lax.axis_index("stream"), lax.axis_index("span")
    per_offset = spans // 2
    lane = lax.broadcasted_iota(jnp.int32, (last - first, LANES), 1)

    def scatter(unit, rank, count, turn):
        values = fresh_ref[unit, first:last, :]
        for h in range(count):
            for k in range(slot):
                shift = shifts_ref[0, (rank + h) * slot + k]
                if turn is not None:
                    shift = (shift + turn) & (LANES - 1)
                moved = pltpu.roll(values, shift, 1)
                spot = bricks_ref.at[columns_ref[0, (rank + h) * slot + k], pl.ds(8 + first, last - first), :]
                pltpu.store(spot, moved, mask=((lane - shift) & (LANES - 2)) == 2 * (slot * h + k))

    @pl.loop(0, OFFSETS * per_offset)
    def _(n):
        stream = here - (n // per_offset - REACH)
        rank = stream * spans + 2 * lax.rem(n, per_offset)

        @pl.when(jnp.logical_and(stream >= 0, stream < streams))
        def _():
            some = jnp.maximum(columns_ref[0, rank * slot], columns_ref[0, (rank + 1) * slot]) > 0

            @pl.when(some)
            def _():
                scatter(n, rank, 2, None)

    opposite = lax.rem(here + streams // 2, streams) * spans + across
    scatter(OFFSETS * per_offset, opposite, 1, 2 * slot * (opposite & 1))


def outer_tiles(size_x, size_y):
    half = size_x // 2
    every = list(range(0, size_y, 8))
    ends = [0, size_y - 8]
    return [(0, every), (half - 1, every)] + [(bx, ends) for bx in (1, 2, half - 3, half - 2)]


def lay_out(bricks_ref, now_ref, bx, tiles):
    half_y = (now_ref.shape[2] - 16) // 2
    for c in range(now_ref.shape[0]):
        for dx in range(2):
            for y in tiles:
                now_ref[c, 2 * bx + dx + 2, 8 + y : 16 + y, :] = cells(bricks_ref, c, dx, bx * half_y + y // 2)


def fill_kernel(
    tables_hbm, frac_ref, jac_ref, base_hbm, near_ref,
    bricks_ref, fresh_ref, now_ref, first_add_ref, second_add_ref,
    spread_ref, flip_ref, columns_ref, shifts_ref, table_sems, brick_sems,
    *, streams, spans, slot
):
    chans = now_ref.shape[0]
    size_x, size_y, size_z = now_ref.shape[1] - 4, now_ref.shape[2] - 16, now_ref.shape[3]
    half_y = size_y // 2
    rows = 8 * chans
    ranks = streams * spans // 2
    here, across = lax.axis_index("stream"), lax.axis_index("span")
    split = -(-rows // 16) * 8
    quarter = size_x // 2 * half_y // 4
    loads = []
    for n, (start, stop) in enumerate(((0, split), (split, rows))):
        for m in range(4):
            inner = (pl.ds(1 + m * quarter, quarter), pl.ds(8 + start, stop - start))
            loads.append(pltpu.make_async_copy(base_hbm.at[inner], bricks_ref.at[inner], brick_sems.at[4 * n + m]))
            loads[-1].start()
    tables = (columns_ref, shifts_ref)
    table_copies = load_tables(tables_hbm, tables, table_sems)

    source = lax.broadcasted_iota(jnp.int32, (LANES // 2, LANES), 0)
    copies = (source == lane_pairs(LANES // 2)).astype(jnp.float32)
    spread_ref[...] = jnp.dot(
        frac_ref[...], copies, preferred_element_type=jnp.float32, precision=lax.Precision.HIGHEST
    )
    cube = (rows // 8, 8, LANES)
    sub = lax.broadcasted_iota(jnp.int32, cube, 1)
    lane = lax.broadcasted_iota(jnp.int32, cube, 2)

    wide = lax.broadcasted_iota(jnp.int32, (8, LANES), 1)

    def turned(group, members):
        flip = flip_ref.at[group]
        for h in range(2):
            blocks = []
            for _, rank, count, _ in members:
                packed = [near_ref[rank + min(h, count - 1), q] for q in range(5)]
                blocks.append(unpack_records(packed))
            while len(blocks) < 3:
                blocks.append(blocks[-1])
            for q in range(4):
                a, b, c = (block[q] for block in blocks)
                start = 2 * slot * h + 16 * q
                even = jnp.where(wide < 2 * rows, pltpu.roll(b, rows, 1), pltpu.roll(c, 2 * rows, 1))
                flip[pl.ds(start, 8, stride=2), :] = jnp.where(wide < rows, a, even)
                odd = jnp.where(wide < 2 * rows, b, pltpu.roll(c, rows, 1))
                flip[pl.ds(start + 1, 8, stride=2), :] = jnp.where(wide < rows, pltpu.roll(a, LANES - rows, 1), odd)
        block = flip[...].T
        for n, (unit, rank, _, swap) in enumerate(members):
            interpolated(unit, rank, swap, block[n * rows : (n + 1) * rows].reshape(cube))

    def interpolated(unit, rank, swap, values):
        shifts = []
        for d in range(3):
            line = spread_ref[pl.ds(d * ranks + (rank >> 1), 1), :]
            if swap:
                line = jnp.where((rank & 1) == 1, pltpu.roll(line, LANES // 2, 1), line)
            shifts.append(line.reshape(1, 1, LANES))
        low = (1.0 - shifts[0]) * values + shifts[0] * pltpu.roll(values, 6, 1)
        values = jnp.where((sub & 2) == 0, low, values)
        low = (1.0 - shifts[1]) * values + shifts[1] * pltpu.roll(values, 7, 1)
        values = jnp.where((sub & 1) == 0, low, values)
        low = (1.0 - shifts[2]) * values + shifts[2] * pltpu.roll(values, LANES - 1, 2)
        values = jnp.where((lane & 1) == 0, low, values)
        fresh_ref[unit] = values.reshape(rows, LANES)

    per_offset = spans // 2
    opposite = lax.rem(here + streams // 2, streams) * spans + across
    members = []
    for d in range(OFFSETS):
        rank = jnp.clip(here - (d - REACH), 0, streams - 1) * spans
        for m in range(per_offset):
            members.append((d * per_offset + m, rank + 2 * m, 2, False))
    members.append((OFFSETS * per_offset, opposite, 1, True))
    for start in range(0, len(members), 3):
        turned(start // 3, members[start : start + 3])

    for copy in table_copies:
        copy.wait()
    for load in loads[0:4]:
        load.wait()
    scatter_rows(tables, fresh_ref, bricks_ref, 0, split, streams=streams, spans=spans, slot=slot)
    for load in loads[4:8]:
        load.wait()

    for bx, tiles in outer_tiles(size_x, size_y):
        lay_out(bricks_ref, now_ref, bx, tiles)

    for side, add_ref in zip(stream_sides(), (first_add_ref, second_add_ref)):
        contribute(now_ref, jac_ref, side, add_ref)


def plane_pre(jac_ref, now_ref, bricks_ref, slope_ref, x, put):
    chans, size_y = now_ref.shape[0], now_ref.shape[2] - 16

    def part(c, dx, dy):
        return now_ref[c, x + 2 + dx, 8 + dy : 8 + size_y + dy, :]

    totals = []
    for c in range(chans):
        first = (x >> 1) * (size_y // 2)
        old = [cells(bricks_ref, chans + c, x & 1, first + y // 2) for y in range(0, size_y, 8)]
        totals.append(part(c, 0, 0) * (4.0 / 3.0) - jnp.concatenate(old, 0) * (1.0 / 3.0))
    for d in range(3):
        if d == 0:
            vectors = [8.0 * (part(c, 1, 0) - part(c, -1, 0)) - (part(c, 2, 0) - part(c, -2, 0)) for c in range(chans)]
        elif d == 1:
            vectors = [8.0 * (part(c, 0, 1) - part(c, 0, -1)) - (part(c, 0, 2) - part(c, 0, -2)) for c in range(chans)]
        else:
            vectors = [slope_ref[c, x] for c in range(chans)]
        totals = [total + value for total, value in zip(totals, mix(jac_ref, d, vectors))]
    for v in range(chans):
        put(v, totals[v])


def slope_planes(now_ref, slope_ref, start, count):
    chans, size_y = now_ref.shape[0], now_ref.shape[2] - 16
    slopes = band({1: 8.0, -1: -8.0, 2: -1.0, -2: 1.0}, now_ref.shape[3])
    for x in range(start, start + count):
        plane = now_ref[:, x + 2, 8 : 8 + size_y, :].reshape(chans * size_y, LANES)
        slope_ref[:, x] = along_z(plane, slopes).reshape(chans, size_y, LANES)


def edge_kernel(
    tables_hbm, jac_ref, now_in, bricks_in, fresh_ref, first_mine_ref, second_mine_ref,
    bricks_ref, now_ref, first_ref, second_ref, pre_ref, first_rim_ref, second_rim_ref,
    slope_ref, columns_ref, shifts_ref, table_sems,
    *, streams, spans, slot
):
    del bricks_in, now_in
    tables = (columns_ref, shifts_ref)
    copies = load_tables(tables_hbm, tables, table_sems)
    chans, size_x, size_y = now_ref.shape[0], now_ref.shape[1] - 4, now_ref.shape[2] - 16
    last = size_x - 1
    for x in (0, 1, size_x + 2, size_x + 3):
        now_ref[:, x] = jnp.zeros((chans, size_y + 16, LANES), jnp.float32)
    rim = jnp.zeros((chans, 8, LANES), jnp.float32)
    for x in range(2, size_x + 2):
        now_ref[:, x, 0:8] = rim
        now_ref[:, x, size_y + 8 : size_y + 16] = rim
    done = dict(outer_tiles(size_x, size_y))
    for bx in range(size_x // 2):
        lay_out(bricks_ref, now_ref, bx, [y for y in range(0, size_y, 8) if y not in done.get(bx, [])])
    slope_planes(now_ref, slope_ref, 0, size_x)
    for copy in copies:
        copy.wait()
    rows = 8 * chans
    split = -(-rows // 16) * 8
    scatter_rows(tables, fresh_ref, bricks_ref, split, rows, streams=streams, spans=spans, slot=slot)
    for side, out_ref in zip(stream_sides(), (first_ref, second_ref)):

        @pl.loop(0, 5)
        def _(p):
            def put(v, value):
                out_ref[p, v] = value

            plane_pre(jac_ref, now_ref, bricks_ref, slope_ref, mirrored(p, side, last), put)


    tile = lax.broadcasted_iota(jnp.int32, (8, LANES), 0)

    def put_rows(x, c, low, top, rows_low, rows_top):
        lower = jnp.where(tile == 5, 0.0, jnp.where(tile < 5, low, rows_low))
        upper = jnp.where(tile == 2, 0.0, jnp.where(tile >= 3, top, rows_top))
        first_rim_ref[x, c], second_rim_ref[x, c] = span_pick(upper, lower)

    refs = ((first_ref, first_mine_ref), (second_ref, second_mine_ref))
    for side, (src_ref, mine_ref) in zip(stream_sides(), refs):
        for c in range(chans):
            for p in range(5):
                low, top = src_ref[p, c, 0:8, :], src_ref[p, c, size_y - 8 : size_y, :]
                start = 2 * size_y + 8 * (p // 2)
                mine = mine_ref[c, start : start + 8, :]
                put_rows(mirrored(p, side, last), c, low, top, beyond(mine, p, False), beyond(mine, p, True))

    @pl.loop(0, size_x - 10)
    def _(n):
        def keep(v, value):
            pre_ref[v, n] = value

        plane_pre(jac_ref, now_ref, bricks_ref, slope_ref, n + 5, keep)
        mixed = edge_rows(now_ref, jac_ref, n + 5, size_y)
        for c in range(chans):
            put_rows(n + 5, c, pre_ref[c, n, 0:8, :], pre_ref[c, n, size_y - 8 : size_y, :], mixed[c], mixed[c])


def tie_kernel(add_ref, plane_in, plane_ref):
    del add_ref, plane_in, plane_ref


def relay_kernel(first_add_ref, second_add_ref, first_in, second_in, first_rim_ref, second_rim_ref):
    del first_in, second_in
    chans = first_add_ref.shape[0]
    size_y = (first_add_ref.shape[1] - 24) // 2
    size_x = first_rim_ref.shape[0] - 3
    tile = lax.broadcasted_iota(jnp.int32, (8, LANES), 0)
    sides = stream_sides()
    for c in range(chans):
        for side, add_ref in zip(sides, (first_add_ref, second_add_ref)):
            for p in range(2):
                x = mirrored(p, side, size_x - 1)
                lower = jnp.where(tile < 5, add_ref[c, p * size_y : p * size_y + 8, :], 0.0)
                upper = jnp.where(tile >= 3, add_ref[c, (p + 1) * size_y - 8 : (p + 1) * size_y, :], 0.0)
                first, second = span_pick(upper, lower)
                first_rim_ref[x, c] += first
                second_rim_ref[x, c] += second
        for t in range(3):
            start = 2 * size_y + 8 * t
            blocks = first_add_ref[c, start : start + 8, :], second_add_ref[c, start : start + 8, :]
            left = jnp.where(sides[0] == 0, blocks[0], blocks[1])
            right = pltpu.roll(jnp.where(sides[0] == 0, blocks[1], blocks[0]), 4, 0)
            lower, upper = jnp.where(tile >= 4, left, right), jnp.where(tile < 4, left, right)
            first_rim_ref[size_x + t, c], second_rim_ref[size_x + t, c] = span_pick(upper, lower)


def radial_band(size_z):
    weights = {0: TAPS[0]}
    for s in range(1, 6):
        weights[s] = weights[-s] = TAPS[s]
    return band(weights, size_z)


def near_filter_kernel(
    pre_ref, first_ref, second_ref, first_add_ref, second_add_ref,
    first_rim_ref, second_rim_ref, first_from_ref, second_from_ref,
    out_ref, low_rows_ref, top_rows_ref, ext_ref, smooth_ref, *, spans
):
    chans, size_x, size_y, size_z = out_ref.shape
    across = lax.axis_index("span")
    last = size_x - 1
    top = size_y + 8
    has_lower = (across > 0).astype(jnp.float32)
    has_upper = (across < spans - 1).astype(jnp.float32)
    tile = lax.broadcasted_iota(jnp.int32, (8, LANES), 0)
    for x in [*range(5), *range(size_x + 5, size_x + 10)]:
        ext_ref[:, x] = jnp.zeros((chans, size_y + 16, LANES), jnp.float32)

    def fold(x, c, plane):
        up, low = span_pick(first_from_ref[x, c], second_from_ref[x, c])
        my_upper, my_lower = span_pick(first_rim_ref[x, c], second_rim_ref[x, c])
        ext_ref[c, x + 5, 16 : top - 8, :] = plane[8 : size_y - 8]
        ext_ref[c, x + 5, 8:16, :] = plane[0:8] + jnp.where(tile < 2, low, 0.0)
        ext_ref[c, x + 5, top - 8 : top, :] = plane[size_y - 8 :] + jnp.where(tile >= 6, up, 0.0)
        mine = has_lower * jnp.where(tile >= 6, my_lower, 0.0)
        ext_ref[c, x + 5, 0:8, :] = jnp.where(tile >= 3, low, 0.0) + mine
        mine = has_upper * jnp.where(tile < 2, my_upper, 0.0)
        ext_ref[c, x + 5, top : top + 8, :] = jnp.where(tile < 5, up, 0.0) + mine

    @pl.loop(0, size_x - 10)
    def _(n):
        for c in range(chans):
            fold(n + 5, c, pre_ref[c, n])

    refs = ((first_ref, first_add_ref), (second_ref, second_add_ref))
    for side, (src_ref, add_ref) in zip(stream_sides(), refs):
        for p in range(5):
            for c in range(chans):
                plane = src_ref[p, c]
                if p < 2:
                    plane = plane + add_ref[c, p * size_y : (p + 1) * size_y, :]
                fold(mirrored(p, side, last), c, plane)

    top_rows_ref[...], low_rows_ref[...] = span_pick(
        first_from_ref[size_x : size_x + 3], second_from_ref[size_x : size_x + 3]
    )
    radial = radial_band(size_z)

    @pl.loop(0, size_x, unroll=4)
    def _(x):
        plane = ext_ref[:, x + 5, 8:top, :].reshape(chans * size_y, LANES)
        smooth_ref[:, x] = along_z(plane, radial).reshape(chans, size_y, LANES)

    @pl.loop(0, size_x)
    def _(x):
        for c in range(chans):
            centre = ext_ref[c, x + 5, 8:top, :]
            total = smooth_ref[c, x] + (2.0 * TAPS[0]) * centre
            for s in range(1, 6):
                ring = ext_ref[c, x + 5 + s, 8:top, :] + ext_ref[c, x + 5 - s, 8:top, :]
                ring = ring + (ext_ref[c, x + 5, 8 + s : top + s, :] + ext_ref[c, x + 5, 8 - s : top - s, :])
                total = total + TAPS[s] * ring
            out_ref[c, x] = centre + (SIGMA / 1024.0) * total


def far_filter_kernel(
    part_ref, first_mine_ref, second_mine_ref, first_from_ref, second_from_ref, low_rows_ref, top_rows_ref,
    out_hbm, out_ref, middle_sem, sems, *, streams
):
    chans, size_x, size_y, _ = part_ref.shape
    tile = lax.broadcasted_iota(jnp.int32, (8, LANES), 0)
    here = lax.axis_index("stream")
    last = size_x - 1
    scale = SIGMA / 1024.0
    middle = pl.ds(5, size_x - 10)
    still = pltpu.make_async_copy(part_ref.at[:, middle], out_hbm.at[:, middle], middle_sem)
    still.start()

    sides = stream_sides()

    def put(n, c):
        planes = pl.ds(sides[n] * (size_x - 5), 5)
        return pltpu.make_async_copy(out_ref.at[c, planes], out_hbm.at[c, planes], sems.at[n, c])

    refs = ((first_mine_ref, first_from_ref), (second_mine_ref, second_from_ref))
    for n, (own_ref, from_ref) in enumerate(refs):
        side = sides[n]
        has = jnp.where(side == 0, here > 0, here < streams - 1).astype(jnp.float32)
        for c in range(chans):
            planes = []
            for p in range(5):
                plane = from_ref[p, c]
                if p < 2:
                    plane = plane + has * own_ref[c, p * size_y : (p + 1) * size_y, :]
                low, top = low_rows_ref[p // 2, c], top_rows_ref[p // 2, c]
                low = jnp.where(side == 1, pltpu.roll(low, 4, 0), low)
                top = jnp.where(side == 1, pltpu.roll(top, 4, 0), top)
                low = jnp.where(tile < 2, beyond(low, p, True), 0.0)
                top = jnp.where(tile >= 6, beyond(top, p, False), 0.0)
                plane = [plane[0:8] + low, plane[8 : size_y - 8], plane[size_y - 8 :] + top]
                planes.append(jnp.concatenate(plane, 0))
            for x in range(5):
                total = TAPS[x + 1] * planes[0]
                for p in range(1, 5 - x):
                    total = total + TAPS[x + 1 + p] * planes[p]
                at = mirrored(x, side, last)
                out_ref[c, at] = part_ref[c, at] + scale * total
            put(n, c).start()
    still.wait()
    for n in range(2):
        for c in range(chans):
            put(n, c).wait()


def params(size=VMEM_BYTES):
    return pltpu.CompilerParams(vmem_limit_bytes=size)


def per_device(q_now, q_prev, jacobians, fractions, send_blocks, recv_blocks):
    streams, spans = lax.axis_size("stream"), lax.axis_size("span")
    chans, size_x, size_y, size_z = q_now.shape
    slots = send_blocks.shape[1]
    slot = slots // (streams * spans)
    rows = 8 * chans
    columns = size_x // 2 * (size_y // 2)
    units = (OFFSETS * spans + 2) // 2
    f32 = jnp.float32
    shape = jax.ShapeDtypeStruct
    bricks = shape((columns + 1, rows + 16, LANES), f32)
    store = shape((STORE_BYTES // (4 * LANES * (rows + 16)), rows + 16, LANES), f32)
    packed = shape((streams * spans, 5, 4, LANES), f32)
    tables = shape((STORE_BYTES // (4 * slots), 1, slots), jnp.int32)
    base, near, tables = pl.pallas_call(
        functools.partial(gather_kernel, streams=streams, spans=spans, slot=slot),
        out_shape=[store, packed, tables],
        in_specs=[HBM] * 4,
        out_specs=[HBM] * 3,
        scratch_shapes=[
            pltpu.VMEM((2 * chans, size_x, size_y + 16, LANES), f32),
            pltpu.VMEM(bricks.shape, f32),
            pltpu.VMEM(packed.shape, f32),
            pltpu.VMEM((-(-columns // 3) * LANES, LANES), f32),
            pltpu.VMEM((units, 3 * LANES, LANES), f32),
            pltpu.VMEM((1, slots), jnp.int32),
            pltpu.VMEM((1, slots), jnp.int32),
            pltpu.VMEM((32, slots), jnp.int32),
            pltpu.SMEM((1, slots), jnp.int32),
            pltpu.SMEM((1, slots), jnp.int32),
            pltpu.SemaphoreType.DMA((2, size_x // 2)),
            pltpu.SemaphoreType.DMA,
            pltpu.SemaphoreType.DMA((streams * spans,)),
            pltpu.SemaphoreType.DMA((6,)),
        ],
        compiler_params=params(BIG_VMEM_BYTES),
    )(send_blocks, recv_blocks, q_now, q_prev)

    near = lax.all_to_all(near, ("stream", "span"), split_axis=0, concat_axis=0, tiled=True)

    jac = jacobians * (-1.0 / 36.0)
    frac_rows = 3 * streams * spans // 2
    add = shape((chans, 2 * size_y + 24, LANES), f32)
    bricks, fresh, now, first_mine, second_mine = pl.pallas_call(
        functools.partial(fill_kernel, streams=streams, spans=spans, slot=slot),
        out_shape=[
            bricks, shape((units, rows, LANES), f32), shape((chans, size_x + 4, size_y + 16, LANES), f32), add, add
        ],
        in_specs=[HBM, VMEM, SMEM, HBM, VMEM],
        out_specs=[VMEM] * 5,
        scratch_shapes=[
            pltpu.VMEM((frac_rows, LANES), f32),
            pltpu.VMEM((-(-units // 3), LANES, LANES), f32),
            pltpu.SMEM((1, slots), jnp.int32),
            pltpu.SMEM((1, slots), jnp.int32),
            pltpu.SemaphoreType.DMA((2,)),
            pltpu.SemaphoreType.DMA((8,)),
        ],
        compiler_params=params(),
    )(tables, fractions.reshape(frac_rows, LANES // 2), jac, base, near)

    def swaps(count):
        pairs = [[(i, i + 1) for i in range(start, count - 1, 2)] for start in range(2)]
        return [pair + [(b, a) for a, b in pair] for pair in pairs]

    along_stream, along_span = swaps(streams), swaps(spans)
    first_add = lax.ppermute(first_mine, "stream", along_stream[0])
    second_add = lax.ppermute(second_mine, "stream", along_stream[1])
    side = shape((5, chans, size_y, LANES), f32)
    rim = shape((size_x + 3, chans, 8, LANES), f32)
    _, _, first, second, pre, first_rim, second_rim = pl.pallas_call(
        functools.partial(edge_kernel, streams=streams, spans=spans, slot=slot),
        out_shape=[
            shape(bricks.shape, f32), shape(now.shape, f32), side, side, shape((chans, size_x - 10, size_y, LANES), f32), rim, rim
        ],
        in_specs=[HBM, SMEM] + [VMEM] * 5,
        out_specs=[VMEM] * 7,
        scratch_shapes=[
            pltpu.VMEM((chans, size_x, size_y, LANES), f32),
            pltpu.SMEM((1, slots), jnp.int32),
            pltpu.SMEM((1, slots), jnp.int32),
            pltpu.SemaphoreType.DMA((2,)),
        ],
        input_output_aliases={3: 0, 2: 1},
        compiler_params=params(),
    )(tables, jac, now, bricks, fresh, first_mine, second_mine)
    second = pl.pallas_call(
        tie_kernel,
        out_shape=side,
        in_specs=[ANY, VMEM],
        out_specs=VMEM,
        input_output_aliases={1: 0},
        compiler_params=params(),
    )(first_add, second)
    first_from = lax.ppermute(first, "stream", along_stream[0])
    second_from = lax.ppermute(second, "stream", along_stream[1])
    first_rim, second_rim = pl.pallas_call(
        relay_kernel,
        out_shape=[rim, rim],
        in_specs=[VMEM] * 4,
        out_specs=[VMEM] * 2,
        input_output_aliases={2: 0, 3: 1},
        compiler_params=params(),
    )(first_add, second_add, first_rim, second_rim)
    first_rows = lax.ppermute(first_rim, "span", along_span[0])
    second_rows = lax.ppermute(second_rim, "span", along_span[1])
    rows_shape = shape((3, chans, 8, LANES), f32)
    part, low_rows, top_rows = pl.pallas_call(
        functools.partial(near_filter_kernel, spans=spans),
        out_shape=[shape(q_now.shape, f32), rows_shape, rows_shape],
        in_specs=[VMEM] * 9,
        out_specs=[VMEM] * 3,
        scratch_shapes=[
            pltpu.VMEM((chans, size_x + 10, size_y + 16, LANES), f32),
            pltpu.VMEM(q_now.shape, f32),
        ],
        compiler_params=params(),
    )(pre, first, second, first_add, second_add, first_rim, second_rim, first_rows, second_rows)
    return pl.pallas_call(
        functools.partial(far_filter_kernel, streams=streams),
        out_shape=shape(q_now.shape, f32),
        in_specs=[VMEM] * 7,
        out_specs=HBM,
        scratch_shapes=[
            pltpu.VMEM(q_now.shape, f32),
            pltpu.SemaphoreType.DMA,
            pltpu.SemaphoreType.DMA((2, chans)),
        ],
        compiler_params=params(),
    )(part, first_mine, second_mine, first_from, second_from, low_rows, top_rows)


def solution(mesh):
    in_specs = (
        P(None, "stream", "span", None),
        P(None, "stream", "span", None),
        P(),
        P(None, ("stream", "span"), None),
        P(("stream", "span"), None),
        P(("stream", "span"), None),
    )
    out_specs = P(None, "stream", "span", None)
    return jax.shard_map(
        per_device, mesh=mesh, in_specs=in_specs, out_specs=out_specs, check_vma=False
    )
```

```python
import functools

import jax
import jax.numpy as jnp
from jax import lax
from jax.experimental import pallas as pl
from jax.experimental.pallas import tpu as pltpu
from jax.sharding import PartitionSpec as P

TAPS = [-252.0, 210.0, -120.0, 45.0, -10.0, 1.0]
SIGMA = 0.6
REACH = 2
OFFSETS = 2 * REACH + 1
LANES = 128
VMEM_BYTES = 32 * 1024 * 1024
BIG_VMEM_BYTES = 60 * 1024 * 1024
STORE_BYTES = 40 * 1024 * 1024
VMEM = pl.BlockSpec(memory_space=pltpu.VMEM)
SMEM = pl.BlockSpec(memory_space=pltpu.SMEM)
HBM = pl.BlockSpec(memory_space=pltpu.HBM)
ANY = pl.BlockSpec(memory_space=pl.ANY)


def lane_pairs(rows):
    return lax.broadcasted_iota(jnp.int32, (rows, LANES), 1) >> 1


def pack_records(parts):
    lane = lax.broadcasted_iota(jnp.int32, (8, LANES), 1)
    first = jnp.where(lane < 80, parts[0], pltpu.roll(parts[3], 80, 1))
    second = jnp.where(lane < 112, pltpu.roll(parts[3], 32, 1), pltpu.roll(parts[2], 112, 1))
    second = jnp.where(lane < 80, parts[1], second)
    rest = pltpu.roll(parts[2], 112, 1)
    rest = jnp.where(lane < 64, rest, pltpu.roll(pltpu.roll(rest, 4, 0), 64, 1))
    return first[0:4], first[4:8], second[0:4], second[4:8], rest[0:4]


def unpack_records(pieces):
    lane = lax.broadcasted_iota(jnp.int32, (8, LANES), 1)
    first = jnp.concatenate(pieces[0:2], 0)
    second = jnp.concatenate(pieces[2:4], 0)
    rest = jnp.concatenate([pieces[4], pltpu.roll(pieces[4], 64, 1)], 0)
    third = jnp.where(lane < 16, pltpu.roll(second, 16, 1), pltpu.roll(rest, 16, 1))
    fourth = jnp.where(lane < 48, pltpu.roll(first, 48, 1), pltpu.roll(second, 96, 1))
    return first, second, third, fourth


def turn(rank, ranks):
    return lax.rem(rank + 1, ranks)


def gather_kernel(
    send_hbm, recv_hbm, now_hbm, old_hbm, bricks_hbm, near_hbm, tables_hbm,
    fields_ref, bricks_ref, near_ref, turned_ref, stage_ref, send_ref, recv_ref, spot_ref, spots_ref, shelves_ref,
    load_sems, brick_sems, near_sems, table_sems,
    *, streams, spans, slot
):
    chans, size_x, size_y, size_z = now_hbm.shape
    half_y = size_y // 2
    deep = (size_z // 2).bit_length() - 1
    rows = 8 * chans
    columns = size_x // 2 * half_y
    here, across = lax.axis_index("stream"), lax.axis_index("span")
    ranks_all = streams * spans

    def chunk(n, bx):
        src = (now_hbm, old_hbm)[n].at[:, pl.ds(2 * bx, 2)]
        dst = fields_ref.at[pl.ds(n * chans, chans), pl.ds(2 * bx, 2), pl.ds(8, size_y)]
        return pltpu.make_async_copy(src, dst, load_sems.at[n, bx])

    table = pltpu.make_async_copy(send_hbm, send_ref, table_sems.at[0])
    table.start()
    received = pltpu.make_async_copy(recv_hbm, recv_ref, table_sems.at[3])
    received.start()
    for bx in range(size_x // 2):
        chunk(0, bx).start()
        chunk(1, bx).start()
    table.wait()
    pick = jnp.maximum(send_ref[...], 0)
    column = pick >> deep
    group = (column * 171) >> 9
    spot_ref[0:1, :] = group * LANES + 2 * (pick & (size_z // 2 - 1))
    spot_ref[8:9, :] = (column - 3 * group) * LANES
    tables = [
        pltpu.make_async_copy(spot_ref.at[pl.ds(8 * n, 1)], dst, table_sems.at[n + 1])
        for n, dst in enumerate((spots_ref, shelves_ref))
    ]
    for copy in tables:
        copy.start()
    received.wait()
    target = recv_ref[...]
    slots = lax.broadcasted_iota(jnp.int32, target.shape, 1)
    spot_ref[16:17, :] = (target >> deep) + 1
    spot_ref[24:25, :] = (2 * target - 2 * slots) & (LANES - 1)
    kept = [
        pltpu.make_async_copy(spot_ref.at[pl.ds(8 * n, 1)], dst, table_sems.at[n + 2])
        for n, dst in ((2, tables_hbm.at[0]), (3, tables_hbm.at[1]))
    ]
    for copy in kept:
        copy.start()

    quarter = lax.broadcasted_iota(jnp.int32, (8, LANES), 0) >> 1

    blank = jnp.zeros((LANES - 3 * rows, LANES), jnp.float32)
    turned = 0
    for bx in range(size_x // 2):
        chunk(0, bx).wait()
        chunk(1, bx).wait()
        for by in range(half_y):
            for v in range(rows // 8):
                total = None
                for t in range(4):
                    c, dx = (4 * v + t) // 2, t % 2
                    start = 8 + 2 * by - 2 * t
                    part = fields_ref[c, 2 * bx + dx, start : start + 8, :]
                    total = part if total is None else jnp.where(quarter == t, part, total)
                bricks_ref[bx * half_y + by + 1, 8 * v + 8 : 8 * v + 16, :] = total
        inner = (pl.ds(1 + bx * half_y, half_y), pl.ds(8, rows))
        kept.append(pltpu.make_async_copy(bricks_ref.at[inner], bricks_hbm.at[inner], brick_sems.at[bx]))
        kept[-1].start()
        ready = (bx + 1) * half_y
        while 3 * turned < columns and min(3 * turned + 3, columns) <= ready:
            parts = [bricks_ref[min(3 * turned + r + 1, columns), 8 : 8 + rows, :] for r in range(3)]
            turned_ref[turned * LANES : (turned + 1) * LANES, :] = jnp.concatenate([*parts, blank], 0).T
            turned += 1


    for copy in tables:
        copy.wait()
    lane = lax.broadcasted_iota(jnp.int32, (8, LANES), 1)

    def fetch(ranks, stage):
        stage[...] = jnp.zeros(stage.shape, jnp.float32)
        for h, rank in enumerate(ranks):
            for k in range(slot):
                spot = spots_ref[0, rank * slot + k]
                shelf = shelves_ref[0, rank * slot + k] + 2 * (slot * h + k)
                stage[pl.ds(shelf, 2), :] = turned_ref[pl.ds(spot, 2), :]
        for h, rank in enumerate(ranks):
            parts = []
            for q in range(4):
                start = 2 * slot * h + 16 * q
                even = [stage[pl.ds(r * LANES + start, 8, stride=2), :] for r in range(3)]
                odd = [stage[pl.ds(r * LANES + start + 1, 8, stride=2), :] for r in range(3)]
                even = even[0] + pltpu.roll(even[1], LANES - rows, 1) + pltpu.roll(even[2], LANES - 2 * rows, 1)
                odd = pltpu.roll(odd[0], rows, 1) + odd[1] + pltpu.roll(odd[2], LANES - rows, 1)
                parts.append(jnp.where(lane < rows, even, odd))
            for q, part in enumerate(pack_records(parts)):
                near_ref[rank, q] = part
            pltpu.make_async_copy(near_ref.at[rank], near_hbm.at[turn(rank, ranks_all)], near_sems.at[rank]).start()

    def finish(ranks):
        for rank in ranks:
            pltpu.make_async_copy(near_ref.at[rank], near_hbm.at[turn(rank, ranks_all)], near_sems.at[rank]).wait()

    opposite = lax.rem(here + streams // 2, streams) * spans + across
    per_offset = spans // 2

    def ranks_of(n):
        stream = here + (n // per_offset - REACH)
        first = stream * spans + 2 * lax.rem(n, per_offset)
        return jnp.logical_and(stream >= 0, stream < streams), (first, first + 1)

    @pl.loop(0, OFFSETS * per_offset)
    def _(n):
        inside, ranks = ranks_of(n)

        @pl.when(inside)
        def _():
            fetch(ranks, stage_ref.at[n])

    fetch((opposite,), stage_ref.at[OFFSETS * per_offset])

    @pl.loop(0, OFFSETS * per_offset)
    def _(n):
        inside, ranks = ranks_of(n)

        @pl.when(inside)
        def _():
            finish(ranks)

    finish((opposite,))
    for copy in kept:
        copy.wait()


def band(weights, size):
    row = lax.broadcasted_iota(jnp.int32, (size, size), 0)
    col = lax.broadcasted_iota(jnp.int32, (size, size), 1)
    total = jnp.zeros((size, size), jnp.float32)
    for shift, weight in weights.items():
        total = jnp.where(row - col == shift, weight, total)
    return total.astype(jnp.bfloat16)


def along_z(values, matrix):
    high = values.astype(jnp.bfloat16)
    low = (values - high.astype(jnp.float32)).astype(jnp.bfloat16)
    total = jnp.dot(high, matrix, preferred_element_type=jnp.float32)
    return total + jnp.dot(low, matrix, preferred_element_type=jnp.float32)


def mix(jac_ref, d, vectors):
    result = []
    for v in range(len(vectors)):
        total = jac_ref[d, v, 0] * vectors[0]
        for w in range(1, len(vectors)):
            total = total + jac_ref[d, v, w] * vectors[w]
        result.append(total)
    return result


def edge_rows(now_ref, jac_ref, x, size_y):
    chans = now_ref.shape[0]
    tile = lax.broadcasted_iota(jnp.int32, (8, LANES), 0)
    vectors = []
    for c in range(chans):
        low = now_ref[c, x + 2, 8:16, :]
        top = now_ref[c, x + 2, size_y : size_y + 8, :]
        low_a, low_b = pltpu.roll(low, 7, 0), pltpu.roll(low, 6, 0)
        top_a, top_b = pltpu.roll(top, 1, 0), pltpu.roll(top, 2, 0)
        value = jnp.where(tile == 7, 8.0 * low_a - low_b, jnp.where(tile == 6, -low_b, 0.0))
        value = jnp.where(tile == 0, top_b - 8.0 * top_a, jnp.where(tile == 1, top_b, value))
        vectors.append(value)
    return mix(jac_ref, 1, vectors)


def mirrored(p, side, last):
    return p + side * (last - 2 * p)


def stream_sides():
    odd = lax.axis_index("stream") & 1
    return 1 - odd, odd


def span_pick(above, below):
    even = (lax.axis_index("span") & 1) == 0
    return jnp.where(even, above, below), jnp.where(even, below, above)


def edge_planes(now_ref, jac_ref, side, start, stop):
    chans = now_ref.shape[0]
    last = now_ref.shape[1] - 5

    def plane(p):
        return mix(jac_ref, 0, [now_ref[c, mirrored(p, side, last) + 2, 8 + start : 8 + stop, :] for c in range(chans)])

    first, second = plane(0), plane(1)
    sign = (1 - 2 * side).astype(jnp.float32)
    return [sign * (8.0 * first[c] - second[c]) for c in range(chans)], [-sign * first[c] for c in range(chans)]


def contribute(now_ref, jac_ref, side, out_ref):
    chans = now_ref.shape[0]
    size_y = now_ref.shape[2] - 16
    last = now_ref.shape[1] - 5
    planes = edge_planes(now_ref, jac_ref, side, 0, size_y)
    tile = lax.broadcasted_iota(jnp.int32, (8, LANES), 0)
    outer = jnp.logical_or(tile < 2, tile >= 6)
    mixed = [edge_rows(now_ref, jac_ref, mirrored(p, side, last), size_y) for p in range(5)]
    for c in range(chans):
        for p in range(2):
            out_ref[c, p * size_y : (p + 1) * size_y, :] = planes[p][c]
        for t in range(3):
            start = 2 * size_y + 8 * t
            if t < 2:
                second = mixed[2 * t + 1][c]
                second = jnp.where(tile < 4, pltpu.roll(second, 2, 0), pltpu.roll(second, 6, 0))
                out_ref[c, start : start + 8, :] = jnp.where(outer, mixed[2 * t][c], second)
            else:
                out_ref[c, start : start + 8, :] = jnp.where(outer, mixed[2 * t][c], 0.0)


def beyond(block, p, lower):
    if p % 2 == 0:
        return block
    return pltpu.roll(block, 6 if lower else 2, 0)


def cells(bricks_ref, c, dx, column):
    quarter = lax.broadcasted_iota(jnp.int32, (8, LANES), 0) >> 1
    total = None
    for s in range(4):
        start = 8 + 4 * c + 2 * dx - 2 * s
        part = bricks_ref[column + s + 1, pl.ds(start, 8), :]
        total = part if total is None else jnp.where(quarter == s, part, total)
    return total


def load_tables(tables_hbm, tables, sems):
    copies = [pltpu.make_async_copy(tables_hbm.at[n], dst, sems.at[n]) for n, dst in enumerate(tables)]
    for copy in copies:
        copy.start()
    return copies


def scatter_rows(tables, fresh_ref, bricks_ref, first, last, *, streams, spans, slot):
    columns_ref, shifts_ref = tables
    here, across = lax.axis_index("stream"), lax.axis_index("span")
    per_offset = spans // 2
    lane = lax.broadcasted_iota(jnp.int32, (last - first, LANES), 1)

    def scatter(unit, rank, count, turn):
        values = fresh_ref[unit, first:last, :]
        for h in range(count):
            for k in range(slot):
                shift = shifts_ref[0, (rank + h) * slot + k]
                if turn is not None:
                    shift = (shift + turn) & (LANES - 1)
                moved = pltpu.roll(values, shift, 1)
                spot = bricks_ref.at[columns_ref[0, (rank + h) * slot + k], pl.ds(8 + first, last - first), :]
                pltpu.store(spot, moved, mask=((lane - shift) & (LANES - 2)) == 2 * (slot * h + k))

    @pl.loop(0, OFFSETS * per_offset)
    def _(n):
        stream = here - (n // per_offset - REACH)
        rank = stream * spans + 2 * lax.rem(n, per_offset)

        @pl.when(jnp.logical_and(stream >= 0, stream < streams))
        def _():
            some = jnp.maximum(columns_ref[0, rank * slot], columns_ref[0, (rank + 1) * slot]) > 0

            @pl.when(some)
            def _():
                scatter(n, rank, 2, None)

    opposite = lax.rem(here + streams // 2, streams) * spans + across
    scatter(OFFSETS * per_offset, opposite, 1, 2 * slot * (opposite & 1))


def outer_tiles(size_x, size_y):
    half = size_x // 2
    every = list(range(0, size_y, 8))
    ends = [0, size_y - 8]
    return [(0, every), (half - 1, every)] + [(bx, ends) for bx in (1, 2, half - 3, half - 2)]


def lay_out(bricks_ref, now_ref, bx, tiles):
    half_y = (now_ref.shape[2] - 16) // 2
    for c in range(now_ref.shape[0]):
        for dx in range(2):
            for y in tiles:
                now_ref[c, 2 * bx + dx + 2, 8 + y : 16 + y, :] = cells(bricks_ref, c, dx, bx * half_y + y // 2)


def fill_kernel(
    tables_hbm, frac_ref, jac_ref, base_hbm, near_ref,
    bricks_ref, fresh_ref, now_ref, first_add_ref, second_add_ref,
    spread_ref, flip_ref, columns_ref, shifts_ref, table_sems, brick_sems,
    *, streams, spans, slot
):
    chans = now_ref.shape[0]
    size_x, size_y, size_z = now_ref.shape[1] - 4, now_ref.shape[2] - 16, now_ref.shape[3]
    half_y = size_y // 2
    rows = 8 * chans
    ranks = streams * spans // 2
    here, across = lax.axis_index("stream"), lax.axis_index("span")
    split = -(-rows // 16) * 8
    quarter = size_x // 2 * half_y // 4
    loads = []
    for n, (start, stop) in enumerate(((0, split), (split, rows))):
        for m in range(4):
            inner = (pl.ds(1 + m * quarter, quarter), pl.ds(8 + start, stop - start))
            loads.append(pltpu.make_async_copy(base_hbm.at[inner], bricks_ref.at[inner], brick_sems.at[4 * n + m]))
            loads[-1].start()
    tables = (columns_ref, shifts_ref)
    table_copies = load_tables(tables_hbm, tables, table_sems)

    source = lax.broadcasted_iota(jnp.int32, (LANES // 2, LANES), 0)
    copies = (source == lane_pairs(LANES // 2)).astype(jnp.float32)
    spread_ref[...] = jnp.dot(
        frac_ref[...], copies, preferred_element_type=jnp.float32, precision=lax.Precision.HIGHEST
    )
    cube = (rows // 8, 8, LANES)
    sub = lax.broadcasted_iota(jnp.int32, cube, 1)
    lane = lax.broadcasted_iota(jnp.int32, cube, 2)

    wide = lax.broadcasted_iota(jnp.int32, (8, LANES), 1)

    def turned(group, members):
        flip = flip_ref.at[group]
        for h in range(2):
            blocks = []
            for _, rank, count, _ in members:
                packed = [near_ref[turn(rank + min(h, count - 1), 2 * ranks), q] for q in range(5)]
                blocks.append(unpack_records(packed))
            while len(blocks) < 3:
                blocks.append(blocks[-1])
            for q in range(4):
                a, b, c = (block[q] for block in blocks)
                start = 2 * slot * h + 16 * q
                even = jnp.where(wide < 2 * rows, pltpu.roll(b, rows, 1), pltpu.roll(c, 2 * rows, 1))
                flip[pl.ds(start, 8, stride=2), :] = jnp.where(wide < rows, a, even)
                odd = jnp.where(wide < 2 * rows, b, pltpu.roll(c, rows, 1))
                flip[pl.ds(start + 1, 8, stride=2), :] = jnp.where(wide < rows, pltpu.roll(a, LANES - rows, 1), odd)
        block = flip[...].T
        for n, (unit, rank, _, swap) in enumerate(members):
            interpolated(unit, rank, swap, block[n * rows : (n + 1) * rows].reshape(cube))

    def interpolated(unit, rank, swap, values):
        shifts = []
        for d in range(3):
            line = spread_ref[pl.ds(d * ranks + (rank >> 1), 1), :]
            if swap:
                line = jnp.where((rank & 1) == 1, pltpu.roll(line, LANES // 2, 1), line)
            shifts.append(line.reshape(1, 1, LANES))
        low = (1.0 - shifts[0]) * values + shifts[0] * pltpu.roll(values, 6, 1)
        values = jnp.where((sub & 2) == 0, low, values)
        low = (1.0 - shifts[1]) * values + shifts[1] * pltpu.roll(values, 7, 1)
        values = jnp.where((sub & 1) == 0, low, values)
        low = (1.0 - shifts[2]) * values + shifts[2] * pltpu.roll(values, LANES - 1, 2)
        values = jnp.where((lane & 1) == 0, low, values)
        fresh_ref[unit] = values.reshape(rows, LANES)

    per_offset = spans // 2
    opposite = lax.rem(here + streams // 2, streams) * spans + across
    members = []
    for d in range(OFFSETS):
        rank = jnp.clip(here - (d - REACH), 0, streams - 1) * spans
        for m in range(per_offset):
            members.append((d * per_offset + m, rank + 2 * m, 2, False))
    members.append((OFFSETS * per_offset, opposite, 1, True))
    for start in range(0, len(members), 3):
        turned(start // 3, members[start : start + 3])

    for copy in table_copies:
        copy.wait()
    for load in loads[0:4]:
        load.wait()
    scatter_rows(tables, fresh_ref, bricks_ref, 0, split, streams=streams, spans=spans, slot=slot)
    for load in loads[4:8]:
        load.wait()

    for bx, tiles in outer_tiles(size_x, size_y):
        lay_out(bricks_ref, now_ref, bx, tiles)

    for side, add_ref in zip(stream_sides(), (first_add_ref, second_add_ref)):
        contribute(now_ref, jac_ref, side, add_ref)


def plane_pre(jac_ref, now_ref, bricks_ref, slope_ref, x, put):
    chans, size_y = now_ref.shape[0], now_ref.shape[2] - 16

    def part(c, dx, dy):
        return now_ref[c, x + 2 + dx, 8 + dy : 8 + size_y + dy, :]

    totals = []
    for c in range(chans):
        first = (x >> 1) * (size_y // 2)
        old = [cells(bricks_ref, chans + c, x & 1, first + y // 2) for y in range(0, size_y, 8)]
        totals.append(part(c, 0, 0) * (4.0 / 3.0) - jnp.concatenate(old, 0) * (1.0 / 3.0))
    for d in range(3):
        if d == 0:
            vectors = [8.0 * (part(c, 1, 0) - part(c, -1, 0)) - (part(c, 2, 0) - part(c, -2, 0)) for c in range(chans)]
        elif d == 1:
            vectors = [8.0 * (part(c, 0, 1) - part(c, 0, -1)) - (part(c, 0, 2) - part(c, 0, -2)) for c in range(chans)]
        else:
            vectors = [slope_ref[c, x] for c in range(chans)]
        totals = [total + value for total, value in zip(totals, mix(jac_ref, d, vectors))]
    for v in range(chans):
        put(v, totals[v])


def slope_planes(now_ref, slope_ref, start, count):
    chans, size_y = now_ref.shape[0], now_ref.shape[2] - 16
    slopes = band({1: 8.0, -1: -8.0, 2: -1.0, -2: 1.0}, now_ref.shape[3])
    for x in range(start, start + count):
        plane = now_ref[:, x + 2, 8 : 8 + size_y, :].reshape(chans * size_y, LANES)
        slope_ref[:, x] = along_z(plane, slopes).reshape(chans, size_y, LANES)


def edge_kernel(
    tables_hbm, jac_ref, now_in, bricks_in, fresh_ref, first_mine_ref, second_mine_ref,
    bricks_ref, now_ref, first_ref, second_ref, pre_ref, first_rim_ref, second_rim_ref,
    slope_ref, columns_ref, shifts_ref, table_sems,
    *, streams, spans, slot
):
    del bricks_in, now_in
    tables = (columns_ref, shifts_ref)
    copies = load_tables(tables_hbm, tables, table_sems)
    chans, size_x, size_y = now_ref.shape[0], now_ref.shape[1] - 4, now_ref.shape[2] - 16
    last = size_x - 1
    for x in (0, 1, size_x + 2, size_x + 3):
        now_ref[:, x] = jnp.zeros((chans, size_y + 16, LANES), jnp.float32)
    rim = jnp.zeros((chans, 8, LANES), jnp.float32)
    for x in range(2, size_x + 2):
        now_ref[:, x, 0:8] = rim
        now_ref[:, x, size_y + 8 : size_y + 16] = rim
    done = dict(outer_tiles(size_x, size_y))
    for bx in range(size_x // 2):
        lay_out(bricks_ref, now_ref, bx, [y for y in range(0, size_y, 8) if y not in done.get(bx, [])])
    slope_planes(now_ref, slope_ref, 0, size_x)
    for copy in copies:
        copy.wait()
    rows = 8 * chans
    split = -(-rows // 16) * 8
    scatter_rows(tables, fresh_ref, bricks_ref, split, rows, streams=streams, spans=spans, slot=slot)
    for side, out_ref in zip(stream_sides(), (first_ref, second_ref)):

        @pl.loop(0, 5)
        def _(p):
            def put(v, value):
                out_ref[p, v] = value

            plane_pre(jac_ref, now_ref, bricks_ref, slope_ref, mirrored(p, side, last), put)


    tile = lax.broadcasted_iota(jnp.int32, (8, LANES), 0)

    def put_rows(x, c, low, top, rows_low, rows_top):
        lower = jnp.where(tile == 5, 0.0, jnp.where(tile < 5, low, rows_low))
        upper = jnp.where(tile == 2, 0.0, jnp.where(tile >= 3, top, rows_top))
        first_rim_ref[x, c], second_rim_ref[x, c] = span_pick(upper, lower)

    refs = ((first_ref, first_mine_ref), (second_ref, second_mine_ref))
    for side, (src_ref, mine_ref) in zip(stream_sides(), refs):
        for c in range(chans):
            for p in range(5):
                low, top = src_ref[p, c, 0:8, :], src_ref[p, c, size_y - 8 : size_y, :]
                start = 2 * size_y + 8 * (p // 2)
                mine = mine_ref[c, start : start + 8, :]
                put_rows(mirrored(p, side, last), c, low, top, beyond(mine, p, False), beyond(mine, p, True))

    @pl.loop(0, size_x - 10)
    def _(n):
        def keep(v, value):
            pre_ref[v, n] = value

        plane_pre(jac_ref, now_ref, bricks_ref, slope_ref, n + 5, keep)
        mixed = edge_rows(now_ref, jac_ref, n + 5, size_y)
        for c in range(chans):
            put_rows(n + 5, c, pre_ref[c, n, 0:8, :], pre_ref[c, n, size_y - 8 : size_y, :], mixed[c], mixed[c])


def tie_kernel(add_ref, plane_in, plane_ref):
    del add_ref, plane_in, plane_ref


def relay_kernel(first_add_ref, second_add_ref, first_in, second_in, first_rim_ref, second_rim_ref):
    del first_in, second_in
    chans = first_add_ref.shape[0]
    size_y = (first_add_ref.shape[1] - 24) // 2
    size_x = first_rim_ref.shape[0] - 3
    tile = lax.broadcasted_iota(jnp.int32, (8, LANES), 0)
    sides = stream_sides()
    for c in range(chans):
        for side, add_ref in zip(sides, (first_add_ref, second_add_ref)):
            for p in range(2):
                x = mirrored(p, side, size_x - 1)
                lower = jnp.where(tile < 5, add_ref[c, p * size_y : p * size_y + 8, :], 0.0)
                upper = jnp.where(tile >= 3, add_ref[c, (p + 1) * size_y - 8 : (p + 1) * size_y, :], 0.0)
                first, second = span_pick(upper, lower)
                first_rim_ref[x, c] += first
                second_rim_ref[x, c] += second
        for t in range(3):
            start = 2 * size_y + 8 * t
            blocks = first_add_ref[c, start : start + 8, :], second_add_ref[c, start : start + 8, :]
            left = jnp.where(sides[0] == 0, blocks[0], blocks[1])
            right = pltpu.roll(jnp.where(sides[0] == 0, blocks[1], blocks[0]), 4, 0)
            lower, upper = jnp.where(tile >= 4, left, right), jnp.where(tile < 4, left, right)
            first_rim_ref[size_x + t, c], second_rim_ref[size_x + t, c] = span_pick(upper, lower)


def radial_band(size_z):
    weights = {0: TAPS[0]}
    for s in range(1, 6):
        weights[s] = weights[-s] = TAPS[s]
    return band(weights, size_z)


def near_filter_kernel(
    pre_ref, first_ref, second_ref, first_add_ref, second_add_ref,
    first_rim_ref, second_rim_ref, first_from_ref, second_from_ref,
    out_ref, low_rows_ref, top_rows_ref, ext_ref, smooth_ref, *, spans
):
    chans, size_x, size_y, size_z = out_ref.shape
    across = lax.axis_index("span")
    last = size_x - 1
    top = size_y + 8
    has_lower = (across > 0).astype(jnp.float32)
    has_upper = (across < spans - 1).astype(jnp.float32)
    tile = lax.broadcasted_iota(jnp.int32, (8, LANES), 0)
    for x in [*range(5), *range(size_x + 5, size_x + 10)]:
        ext_ref[:, x] = jnp.zeros((chans, size_y + 16, LANES), jnp.float32)

    def fold(x, c, plane):
        up, low = span_pick(first_from_ref[x, c], second_from_ref[x, c])
        my_upper, my_lower = span_pick(first_rim_ref[x, c], second_rim_ref[x, c])
        ext_ref[c, x + 5, 16 : top - 8, :] = plane[8 : size_y - 8]
        ext_ref[c, x + 5, 8:16, :] = plane[0:8] + jnp.where(tile < 2, low, 0.0)
        ext_ref[c, x + 5, top - 8 : top, :] = plane[size_y - 8 :] + jnp.where(tile >= 6, up, 0.0)
        mine = has_lower * jnp.where(tile >= 6, my_lower, 0.0)
        ext_ref[c, x + 5, 0:8, :] = jnp.where(tile >= 3, low, 0.0) + mine
        mine = has_upper * jnp.where(tile < 2, my_upper, 0.0)
        ext_ref[c, x + 5, top : top + 8, :] = jnp.where(tile < 5, up, 0.0) + mine

    @pl.loop(0, size_x - 10)
    def _(n):
        for c in range(chans):
            fold(n + 5, c, pre_ref[c, n])

    refs = ((first_ref, first_add_ref), (second_ref, second_add_ref))
    for side, (src_ref, add_ref) in zip(stream_sides(), refs):
        for p in range(5):
            for c in range(chans):
                plane = src_ref[p, c]
                if p < 2:
                    plane = plane + add_ref[c, p * size_y : (p + 1) * size_y, :]
                fold(mirrored(p, side, last), c, plane)

    top_rows_ref[...], low_rows_ref[...] = span_pick(
        first_from_ref[size_x : size_x + 3], second_from_ref[size_x : size_x + 3]
    )
    radial = radial_band(size_z)

    @pl.loop(0, size_x, unroll=4)
    def _(x):
        plane = ext_ref[:, x + 5, 8:top, :].reshape(chans * size_y, LANES)
        smooth_ref[:, x] = along_z(plane, radial).reshape(chans, size_y, LANES)

    @pl.loop(0, size_x)
    def _(x):
        for c in range(chans):
            centre = ext_ref[c, x + 5, 8:top, :]
            total = smooth_ref[c, x] + (2.0 * TAPS[0]) * centre
            for s in range(1, 6):
                ring = ext_ref[c, x + 5 + s, 8:top, :] + ext_ref[c, x + 5 - s, 8:top, :]
                ring = ring + (ext_ref[c, x + 5, 8 + s : top + s, :] + ext_ref[c, x + 5, 8 - s : top - s, :])
                total = total + TAPS[s] * ring
            out_ref[c, x] = centre + (SIGMA / 1024.0) * total


def far_filter_kernel(
    part_ref, first_mine_ref, second_mine_ref, first_from_ref, second_from_ref, low_rows_ref, top_rows_ref,
    out_hbm, out_ref, middle_sem, sems, *, streams
):
    chans, size_x, size_y, _ = part_ref.shape
    tile = lax.broadcasted_iota(jnp.int32, (8, LANES), 0)
    here = lax.axis_index("stream")
    last = size_x - 1
    scale = SIGMA / 1024.0
    middle = pl.ds(5, size_x - 10)
    still = pltpu.make_async_copy(part_ref.at[:, middle], out_hbm.at[:, middle], middle_sem)
    still.start()

    sides = stream_sides()

    def put(n, c):
        planes = pl.ds(sides[n] * (size_x - 5), 5)
        return pltpu.make_async_copy(out_ref.at[c, planes], out_hbm.at[c, planes], sems.at[n, c])

    refs = ((first_mine_ref, first_from_ref), (second_mine_ref, second_from_ref))
    for n, (own_ref, from_ref) in enumerate(refs):
        side = sides[n]
        has = jnp.where(side == 0, here > 0, here < streams - 1).astype(jnp.float32)
        for c in range(chans):
            planes = []
            for p in range(5):
                plane = from_ref[p, c]
                if p < 2:
                    plane = plane + has * own_ref[c, p * size_y : (p + 1) * size_y, :]
                low, top = low_rows_ref[p // 2, c], top_rows_ref[p // 2, c]
                low = jnp.where(side == 1, pltpu.roll(low, 4, 0), low)
                top = jnp.where(side == 1, pltpu.roll(top, 4, 0), top)
                low = jnp.where(tile < 2, beyond(low, p, True), 0.0)
                top = jnp.where(tile >= 6, beyond(top, p, False), 0.0)
                plane = [plane[0:8] + low, plane[8 : size_y - 8], plane[size_y - 8 :] + top]
                planes.append(jnp.concatenate(plane, 0))
            for x in range(5):
                total = TAPS[x + 1] * planes[0]
                for p in range(1, 5 - x):
                    total = total + TAPS[x + 1 + p] * planes[p]
                at = mirrored(x, side, last)
                out_ref[c, at] = part_ref[c, at] + scale * total
            put(n, c).start()
    still.wait()
    for n in range(2):
        for c in range(chans):
            put(n, c).wait()


def params(size=VMEM_BYTES):
    return pltpu.CompilerParams(vmem_limit_bytes=size)


def per_device(q_now, q_prev, jacobians, fractions, send_blocks, recv_blocks):
    streams, spans = lax.axis_size("stream"), lax.axis_size("span")
    chans, size_x, size_y, size_z = q_now.shape
    slots = send_blocks.shape[1]
    slot = slots // (streams * spans)
    rows = 8 * chans
    columns = size_x // 2 * (size_y // 2)
    units = (OFFSETS * spans + 2) // 2
    f32 = jnp.float32
    shape = jax.ShapeDtypeStruct
    bricks = shape((columns + 1, rows + 16, LANES), f32)
    store = shape((STORE_BYTES // (4 * LANES * (rows + 16)), rows + 16, LANES), f32)
    packed = shape((streams * spans, 5, 4, LANES), f32)
    tables = shape((STORE_BYTES // (4 * slots), 1, slots), jnp.int32)
    base, near, tables = pl.pallas_call(
        functools.partial(gather_kernel, streams=streams, spans=spans, slot=slot),
        out_shape=[store, packed, tables],
        in_specs=[HBM] * 4,
        out_specs=[HBM] * 3,
        scratch_shapes=[
            pltpu.VMEM((2 * chans, size_x, size_y + 16, LANES), f32),
            pltpu.VMEM(bricks.shape, f32),
            pltpu.VMEM(packed.shape, f32),
            pltpu.VMEM((-(-columns // 3) * LANES, LANES), f32),
            pltpu.VMEM((units, 3 * LANES, LANES), f32),
            pltpu.VMEM((1, slots), jnp.int32),
            pltpu.VMEM((1, slots), jnp.int32),
            pltpu.VMEM((32, slots), jnp.int32),
            pltpu.SMEM((1, slots), jnp.int32),
            pltpu.SMEM((1, slots), jnp.int32),
            pltpu.SemaphoreType.DMA((2, size_x // 2)),
            pltpu.SemaphoreType.DMA((size_x // 2,)),
            pltpu.SemaphoreType.DMA((streams * spans,)),
            pltpu.SemaphoreType.DMA((6,)),
        ],
        compiler_params=params(BIG_VMEM_BYTES),
    )(send_blocks, recv_blocks, q_now, q_prev)

    ranks = streams * spans
    places = [[(place - 1) % ranks for place in range(ranks)]]
    axes = ("stream", "span")
    near = lax.all_to_all(near, axes, split_axis=0, concat_axis=0, tiled=True, axis_index_groups=places)

    jac = jacobians * (-1.0 / 36.0)
    frac_rows = 3 * streams * spans // 2
    add = shape((chans, 2 * size_y + 24, LANES), f32)
    bricks, fresh, now, first_mine, second_mine = pl.pallas_call(
        functools.partial(fill_kernel, streams=streams, spans=spans, slot=slot),
        out_shape=[
            bricks, shape((units, rows, LANES), f32), shape((chans, size_x + 4, size_y + 16, LANES), f32), add, add
        ],
        in_specs=[HBM, VMEM, SMEM, HBM, VMEM],
        out_specs=[VMEM] * 5,
        scratch_shapes=[
            pltpu.VMEM((frac_rows, LANES), f32),
            pltpu.VMEM((-(-units // 3), LANES, LANES), f32),
            pltpu.SMEM((1, slots), jnp.int32),
            pltpu.SMEM((1, slots), jnp.int32),
            pltpu.SemaphoreType.DMA((2,)),
            pltpu.SemaphoreType.DMA((8,)),
        ],
        compiler_params=params(),
    )(tables, fractions.reshape(frac_rows, LANES // 2), jac, base, near)

    def swaps(count):
        pairs = [[(i, i + 1) for i in range(start, count - 1, 2)] for start in range(2)]
        return [pair + [(b, a) for a, b in pair] for pair in pairs]

    along_stream, along_span = swaps(streams), swaps(spans)
    first_add = lax.ppermute(first_mine, "stream", along_stream[0])
    second_add = lax.ppermute(second_mine, "stream", along_stream[1])
    side = shape((5, chans, size_y, LANES), f32)
    rim = shape((size_x + 3, chans, 8, LANES), f32)
    _, _, first, second, pre, first_rim, second_rim = pl.pallas_call(
        functools.partial(edge_kernel, streams=streams, spans=spans, slot=slot),
        out_shape=[
            shape(bricks.shape, f32), shape(now.shape, f32), side, side, shape((chans, size_x - 10, size_y, LANES), f32), rim, rim
        ],
        in_specs=[HBM, SMEM] + [VMEM] * 5,
        out_specs=[VMEM] * 7,
        scratch_shapes=[
            pltpu.VMEM((chans, size_x, size_y, LANES), f32),
            pltpu.SMEM((1, slots), jnp.int32),
            pltpu.SMEM((1, slots), jnp.int32),
            pltpu.SemaphoreType.DMA((2,)),
        ],
        input_output_aliases={3: 0, 2: 1},
        compiler_params=params(),
    )(tables, jac, now, bricks, fresh, first_mine, second_mine)
    second = pl.pallas_call(
        tie_kernel,
        out_shape=side,
        in_specs=[ANY, VMEM],
        out_specs=VMEM,
        input_output_aliases={1: 0},
        compiler_params=params(),
    )(first_add, second)
    first_from = lax.ppermute(first, "stream", along_stream[0])
    second_from = lax.ppermute(second, "stream", along_stream[1])
    first_rim, second_rim = pl.pallas_call(
        relay_kernel,
        out_shape=[rim, rim],
        in_specs=[VMEM] * 4,
        out_specs=[VMEM] * 2,
        input_output_aliases={2: 0, 3: 1},
        compiler_params=params(),
    )(first_add, second_add, first_rim, second_rim)
    first_rows = lax.ppermute(first_rim, "span", along_span[0])
    second_rows = lax.ppermute(second_rim, "span", along_span[1])
    rows_shape = shape((3, chans, 8, LANES), f32)
    part, low_rows, top_rows = pl.pallas_call(
        functools.partial(near_filter_kernel, spans=spans),
        out_shape=[shape(q_now.shape, f32), rows_shape, rows_shape],
        in_specs=[VMEM] * 9,
        out_specs=[VMEM] * 3,
        scratch_shapes=[
            pltpu.VMEM((chans, size_x + 10, size_y + 16, LANES), f32),
            pltpu.VMEM(q_now.shape, f32),
        ],
        compiler_params=params(),
    )(pre, first, second, first_add, second_add, first_rim, second_rim, first_rows, second_rows)
    return pl.pallas_call(
        functools.partial(far_filter_kernel, streams=streams),
        out_shape=shape(q_now.shape, f32),
        in_specs=[VMEM] * 7,
        out_specs=HBM,
        scratch_shapes=[
            pltpu.VMEM(q_now.shape, f32),
            pltpu.SemaphoreType.DMA,
            pltpu.SemaphoreType.DMA((2, chans)),
        ],
        compiler_params=params(),
    )(part, first_mine, second_mine, first_from, second_from, low_rows, top_rows)


def solution(mesh):
    in_specs = (
        P(None, "stream", "span", None),
        P(None, "stream", "span", None),
        P(),
        P(None, ("stream", "span"), None),
        P(("stream", "span"), None),
        P(("stream", "span"), None),
    )
    out_specs = P(None, "stream", "span", None)
    return jax.shard_map(
        per_device, mesh=mesh, in_specs=in_specs, out_specs=out_specs, check_vma=False
    )
```
